256 devices in a mesh: row: 8 (over y, core), col: 32 (over z, x).
Axes of the slice: x: 4, y: 4, z: 8, core: 2. Of those that a mesh axis runs over, the one named last changes fastest.
Arguments:
- raw_blocks: bfloat16 [2, 16384, 16384], P(None, 'row', 'col'), may hold values from -1.25 to 1.25
- occupancy: int32 [32, 16384], P('row', 'col'), may hold values 0 or 1
- exponent: int32 [32, 32], P('row', 'col'), may hold values from -2 to 2
Outputs:
- multiples: bfloat16 [2, 2, 16384, 512], P(None, None, ('row', 'col'))
The draws below stay inside these ranges and needn't reach their ends.
All inputs are finite; a program needn't handle non-finite values. No bound on the sum of `occupancy` on one device may be relied on, other than what follows from the above.
Results may differ from the reference program's by a relative error of at most 0.02.
Values may be sent and summed in bfloat16 or wider, within the bound.
A program may use at most 64 MiB of HBM per device.

```python
import jax
import jax.numpy as jnp
from jax import lax

COLS_DEV = 512
TILE = 512
TRACES = 16384
N_COL = 32


def plant(drawn, key, least, top_value):
    longest = drawn.shape.index(max(drawn.shape))
    spots = []
    for shift in (0, 1):
        where = [jax.random.randint(jax.random.fold_in(key, axis), (), 0, length) for axis, length in enumerate(drawn.shape)]
        where[longest] = (where[longest] + shift) % drawn.shape[longest]
        spots.append(tuple(where))
    return drawn.at[spots[0]].set(least).at[spots[1]].set(top_value)


def spiked(entries, stream_key, source, target, parts, factor):
    owner, partner = [(jnp.arange(entries.shape[dim]) // (entries.shape[dim] // parts)).reshape([-1 if axis == dim else 1 for axis in range(entries.ndim)]) for dim in (source, target)]
    chosen = jax.random.permutation(stream_key, parts)[partner]
    strong = (owner == chosen) | (owner == (partner + parts // 2) % parts)
    return jnp.where(strong, factor * entries, entries)


def levels(rng, shape, cuts, low, top_value):
    loudness, own = 1.0, jax.random.fold_in(rng, 6)
    for position, blocks in cuts:
        draws = jnp.exp(jax.random.uniform(jax.random.fold_in(own, position), (blocks,), jnp.float32, low / len(cuts), top_value / len(cuts)))
        loudness = loudness * jnp.repeat(draws, shape[position] // blocks).reshape([-1 if axis == position else 1 for axis in range(len(shape))])
    return loudness


def heavy_noise(key, shape, spread, reach, pieces, heavy, kind=jnp.bfloat16):
    array = spread * jax.random.normal(key, shape, jnp.float32)
    if pieces:
        array = array * levels(key, shape, pieces, -0.22, 0.18)
    return jnp.clip(spiked(array, jax.random.fold_in(key, 3), *heavy), -reach, reach).astype(kind)


def setup_inputs(seed: int = 0) -> dict:
    streams_of = jax.random.split(jax.random.key(seed), 4)
    raw_blocks = heavy_noise(streams_of[0], (2, TRACES, TRACES), (0.5 * TRACES ** -0.25), 1.25, ((1, 8), (2, 32)), (2, 1, 32, 2.75))
    occupancy = plant((jax.random.randint(streams_of[1], (TRACES // TILE, TRACES), 0, 4) < 3).astype(jnp.int32), jax.random.fold_in(streams_of[1], 1), 0, 1)
    exponent = plant(jax.random.randint(streams_of[2], (TRACES // TILE, TRACES // TILE), -2, 3), jax.random.fold_in(streams_of[2], 1), -2, 2).astype(jnp.int32)
    return {"raw_blocks": raw_blocks, "occupancy": occupancy, "exponent": exponent}


def decode(raw_blocks, occupancy, exponent):
    tile_scale = jnp.exp2(exponent.astype(jnp.float32))
    col_scale = jnp.repeat(tile_scale, TILE, axis=1)
    factor = occupancy.astype(jnp.float32) * col_scale
    shaped = raw_blocks.astype(jnp.float32).reshape(2, TRACES // TILE, TILE, TRACES) * factor[None, :, None, :]
    return shaped.reshape(2, TRACES, TRACES).astype(jnp.bfloat16)


def hdot(left_op, right_op):
    return jnp.dot(left_op, right_op, precision=lax.Precision.HIGHEST, preferred_element_type=jnp.float32)


def reference(raw_blocks, occupancy, exponent):
    decoded = decode(raw_blocks, occupancy, exponent)
    panels_out = []
    for which_panel in range(2):
        offset = which_panel * (TRACES // 2)
        panel_cols = lax.dynamic_slice_in_dim(decoded, offset, COLS_DEV, 2).astype(jnp.float32)

        def add_block(running, block_idx):
            left_op = lax.dynamic_slice_in_dim(decoded, (block_idx * COLS_DEV).astype(jnp.int32), COLS_DEV, 2).astype(jnp.float32)
            right_op = lax.dynamic_slice_in_dim(panel_cols, (block_idx * COLS_DEV).astype(jnp.int32), COLS_DEV, 1)
            real_part = hdot(left_op[0], right_op[0]) - hdot(left_op[1], right_op[1])
            imag_part = hdot(left_op[0], right_op[1]) + hdot(left_op[1], right_op[0])
            partial_value = lax.optimization_barrier(jnp.stack([real_part, imag_part]).astype(jnp.bfloat16))
            return running + partial_value.astype(jnp.float32), None

        running, _ = lax.scan(add_block, jnp.zeros((2, TRACES, COLS_DEV), jnp.float32), jnp.arange(N_COL, dtype=jnp.int32))
        panels_out.append(running.astype(jnp.bfloat16))
    return jnp.stack(panels_out)
```

```python
import functools

import jax
import jax.numpy as jnp
from jax import lax
from jax.experimental import pallas as pl
from jax.experimental.pallas import tpu as pltpu
from jax.sharding import PartitionSpec as P

MESH = pl.DeviceIdType.MESH
NY, NZ, NX = 4, 8, 4
WAVES = 4
LANES = 128
SPAN = 3


def wrap(index, size):
    return lax.rem(index + size, size)


class Chain:
    def __init__(self, n, me, neighbour, own, groups, send, recv, send_sem, recv_sem):
        self.n, self.me, self.neighbour, self.own, self.groups = n, me, neighbour, own, groups
        self.send, self.recv, self.send_sem, self.recv_sem = send, recv, send_sem, recv_sem
        self.started = []

    def half(self, side):
        size = self.groups // 2
        return pl.ds(size * side, size)

    def copy(self, side, step):
        if step == 0:
            cut = self.half(side)
            source, target = self.send.at[side, 0, cut], self.recv.at[side, 0, cut]
        else:
            source, target = self.send.at[side, step], self.recv.at[side, step]
        return pltpu.make_async_remote_copy(
            src_ref=source,
            dst_ref=target,
            send_sem=self.send_sem.at[side, step],
            recv_sem=self.recv_sem.at[side, step],
            device_id=self.neighbour(1 - 2 * side),
            device_id_type=MESH,
        )

    def step(self, step):
        for side in range(2):
            away = self.n // 2 - step
            dest = wrap(self.me + (1 - 2 * side) * away, self.n)
            size = self.groups // 2
            halves = (side, 1 - side) if step else (side,)
            if step:
                self.copy(side, step - 1).wait_recv()
            for part in halves:
                with_received = step > 1 or (step == 1 and part == side)

                def block(g, _, part=part, with_received=with_received, dest=dest, side=side):
                    at = part * size + g
                    value = self.own(dest, at)
                    if with_received:
                        value = value + self.recv[side, step - 1, at].astype(jnp.float32)
                    self.send[side, step, at] = value.astype(jnp.bfloat16)
                    return _

                lax.fori_loop(0, size, block, 0)
            copy = self.copy(side, step)
            copy.start()
            self.started.append(copy)

    def finish(self, put):
        last = self.n // 2 - 1
        for side in range(2):
            self.copy(side, last).wait_recv()

        def block(g, _):
            value = self.own(self.me, g)
            for side in range(2):
                value = value + self.recv[side, last, g].astype(jnp.float32)
            put(g, value)
            return _

        lax.fori_loop(0, self.groups, block, 0)

    def drain(self):
        for copy in self.started:
            copy.wait_send()


def kernel(
    raw_ref, occ_ref, exp_ref, out_ref,
    raw, factor, mine, land, rhs, part, summed,
    z_send, z_recv, x_send, x_recv, zx_send, zx_recv, xz_send, xz_recv,
    raw_sem, root_sem, land_sem, pass_sem,
    z_ss, z_rs, x_ss, x_rs, zx_ss, zx_rs, xz_ss, xz_rs,
):
    row, col = lax.axis_index("row"), lax.axis_index("col")
    y, core, z, x = row // 2, row % 2, col // NX, col % NX

    def device(y, core, z, x):
        return (wrap(y, NY) * 2 + core, wrap(z, NZ) * NX + wrap(x, NX))

    def along_z(step):
        return device(y, core, z + step, x)

    def along_x(step):
        return device(y, core, z, x + step)

    def along_y(step):
        return device(y + step, core, z, x)

    other = device(y, 1 - core, z, x)
    fetches = [
        pltpu.make_async_copy(
            raw_ref.at[:, :, :, :, pl.ds(LANES * q, LANES)],
            raw.at[:, :, :, :, pl.ds(LANES * q, LANES)],
            raw_sem.at[q],
        )
        for q in range(WAVES)
    ]
    for fetch in fetches:
        fetch.start()

    barrier = pltpu.get_barrier_semaphore()
    for peer in (along_z(1), along_z(-1), along_x(1), along_x(-1), along_y(1), along_y(-1), other):
        pl.semaphore_signal(barrier, inc=1, device_id=peer, device_id_type=MESH)
    expected = jnp.int32(7)
    is_root = [col == p * (NZ * NX // 2) for p in range(2)]
    is_first = row == z
    for p in range(2):
        for j in range(NX):
            target = row * NX + j
            needed = jnp.logical_and(is_root[p], target != col)
            expected = expected + needed.astype(jnp.int32)

            @pl.when(needed)
            def _(target=target):
                pl.semaphore_signal(barrier, inc=1, device_id=(row, target), device_id_type=MESH)

        needed = jnp.logical_and(is_first, jnp.logical_not(is_root[p]))
        expected = expected + needed.astype(jnp.int32)

        @pl.when(needed)
        def _(p=p):
            pl.semaphore_signal(
                barrier, inc=1, device_id=(row, jnp.int32(p * (NZ * NX // 2))), device_id_type=MESH
            )

    exponent = exp_ref[...]
    scale = jnp.full(exponent.shape, 1.0, jnp.float32)
    for power in (-2, -1, 1, 2):
        scale = jnp.where(exponent == power, jnp.float32(2.0**power), scale)
    scaled = occ_ref[...].astype(jnp.float32) * scale
    for tile in range(NZ // 2):
        factor[tile] = scaled[tile : tile + 1]

    def root_copy(p, q, j):
        return pltpu.make_async_remote_copy(
            src_ref=mine.at[pl.ds(2 * j, 2), :, :, pl.ds(2 * LANES * q, 2 * LANES)],
            dst_ref=land.at[p, q],
            send_sem=root_sem.at[q, j],
            recv_sem=land_sem.at[p, q],
            device_id=(row, row * NX + j),
            device_id_type=MESH,
        )

    def stay_copy(p, q):
        return pltpu.make_async_copy(
            mine.at[pl.ds(0, 2), :, :, pl.ds(2 * LANES * q, 2 * LANES)], land.at[p, q], land_sem.at[p, q]
        )

    for q in range(WAVES):
        fetches[q].wait()

        def decode(zd, _, q=q):
            f = factor[zd // 2, :, LANES * q : LANES * (q + 1)]
            for half in range(2):
                value = raw[half, zd, :, :, LANES * q : LANES * (q + 1)].astype(jnp.float32)
                start = 2 * LANES * q + LANES * half
                mine[zd, :, :, start : start + LANES] = (value * f[None]).astype(jnp.bfloat16)
            return _

        lax.fori_loop(0, NZ, decode, 0)
        if q == 0:
            pl.semaphore_wait(barrier, expected)
        for p in range(2):
            for j in range(NX):
                own = row * NX + j == col

                @pl.when(jnp.logical_and(is_root[p], jnp.logical_not(own)))
                def _(p=p, q=q, j=j):
                    root_copy(p, q, j).start()

            @pl.when(jnp.logical_and(is_root[p], is_first))
            def _(p=p, q=q):
                stay_copy(p, q).start()

    match = core == z % 2
    dy = wrap(y - z // 2, NY)

    def passes(p, q):
        forward = jnp.logical_or(dy == 0, dy == (1 if q % 2 == 0 else NY))
        backward = jnp.logical_or(dy == 0, dy == (NY - 1 if q % 2 == 1 else NY))
        for slot, (needed, peer) in enumerate(
            ((forward, along_y(1)), (backward, along_y(-1)), (dy >= 0, other))
        ):
            copy = pltpu.make_async_remote_copy(
                src_ref=land.at[p, q],
                dst_ref=land.at[p, q],
                send_sem=pass_sem.at[p, q, slot],
                recv_sem=land_sem.at[p, q],
                device_id=peer,
                device_id_type=MESH,
            )
            yield jnp.logical_and(match, needed), copy

    def arrive(p, q):
        pltpu.make_async_copy(land.at[p, q], land.at[p, q], land_sem.at[p, q]).wait()
        for needed, copy in passes(p, q):

            @pl.when(needed)
            def _(copy=copy):
                copy.start()

    def build(p, q):
        for k in range(4):
            block = land[p, q, k // 2, 2 * (k % 2) : 2 * (k % 2) + 2].reshape(LANES, 2 * LANES)
            real, imag = block[:, :LANES], block[:, LANES:]
            at = 2 * LANES * k
            rhs[p, at : at + LANES, :] = block
            rhs[p, at + LANES : at + 2 * LANES, :LANES] = -imag
            rhs[p, at + LANES : at + 2 * LANES, LANES:] = real

    def product(p, rows):
        return jnp.dot(rows.reshape(4 * 64, 8 * LANES), rhs[p], preferred_element_type=jnp.float32)

    def multiply_z(slot, start, count):
        def block(k, _):
            zd = wrap(z + NZ // 2 + k, NZ)
            part[slot, 0, zd] = product(0, mine[zd]).reshape(4, 64, 2 * LANES)
            return _

        lax.fori_loop(start, start + count, block, 0)

    def multiply_x(slot, start, count):
        def block(k, _):
            xd = wrap(x + NX // 2 + k // 2, NX)
            rows = pl.ds(4 * (k % 2), 4)
            part[slot, 1, rows, xd] = product(1, mine[rows, xd]).reshape(4, 64, 2 * LANES)
            return _

        lax.fori_loop(start, start + count, block, 0)

    def chains(w):
        slot = w % 2
        first_z = Chain(
            NZ, z, along_z, lambda d, g: part[slot, 0, d, g], NX,
            z_send.at[w], z_recv.at[w], z_ss.at[w], z_rs.at[w],
        )
        first_x = Chain(
            NX, x, along_x, lambda d, g: part[slot, 1, g, d], NZ,
            x_send.at[w], x_recv.at[w], x_ss.at[w], x_rs.at[w],
        )
        then_x = Chain(
            NX, x, along_x, lambda d, g: summed[slot, 0, d, g], 2,
            zx_send.at[w], zx_recv.at[w], zx_ss.at[w], zx_rs.at[w],
        )
        then_z = Chain(
            NZ, z, along_z, lambda d, g: summed[slot, 1, d, g], 2,
            xz_send.at[w], xz_recv.at[w], xz_ss.at[w], xz_rs.at[w],
        )
        return first_z, first_x, then_x, then_z

    all_chains = [chains(w) for w in range(WAVES)]

    def keep(slot, which):
        def put(g, value):
            summed[slot, which, g] = value.reshape(2, 32, 2 * LANES)

        return put

    def result(p, w):
        def put(g, value):
            value = value.astype(jnp.bfloat16)
            for half in range(2):
                out_ref[p, half, pl.ds(pl.multiple_of(32 * g, 32), 32), LANES * w : LANES * (w + 1)] = value[
                    :, LANES * half : LANES * (half + 1)
                ]

        return put

    def run(w, k):
        first_z, first_x, then_x, then_z = all_chains[w]
        slot = w % 2
        if k == 0:
            arrive(0, w)
            arrive(1, w)
            build(0, w)
            multiply_z(slot, 0, 1)
            first_z.step(0)
            build(1, w)
            multiply_x(slot, 0, 2)
            first_x.step(0)
            multiply_z(slot, 1, 7)
            multiply_x(slot, 2, 6)
        if 1 <= k <= 3:
            first_z.step(k)
        if k == 1:
            first_x.step(1)
        if k == 2:
            first_x.finish(keep(slot, 1))
        if 2 <= k <= 5:
            then_z.step(k - 2)
        if k == 4:
            first_z.finish(keep(slot, 0))
        if 4 <= k <= 5:
            then_x.step(k - 4)
        if k == 6:
            then_x.finish(result(0, w))
            then_z.finish(result(1, w))

    for t in range(SPAN * (WAVES - 1) + 7):
        for w in range(WAVES):
            if 0 <= t - SPAN * w <= 6:
                run(w, t - SPAN * w)

    for group in all_chains:
        for chain in group:
            chain.drain()
    for p in range(2):
        for q in range(WAVES):
            for needed, copy in passes(p, q):

                @pl.when(needed)
                def _(copy=copy):
                    copy.wait_send()

            for j in range(NX):

                @pl.when(jnp.logical_and(is_root[p], row * NX + j != col))
                def _(p=p, q=q, j=j):
                    root_copy(p, q, j).wait_send()


def on_device(raw_blocks, occupancy, exponent):
    bf16, f32 = jnp.bfloat16, jnp.float32
    dma = pltpu.SemaphoreType.DMA
    n = 2 * LANES
    return pl.pallas_call(
        kernel,
        out_shape=jax.ShapeDtypeStruct((2, 2, 64, 512), bf16),
        in_specs=[
            pl.BlockSpec(memory_space=pl.ANY),
            pl.BlockSpec(memory_space=pltpu.VMEM),
            pl.BlockSpec(memory_space=pltpu.VMEM),
        ],
        out_specs=pl.BlockSpec(memory_space=pltpu.VMEM),
        scratch_shapes=[
            pltpu.VMEM((2, NZ, NX, 64, 512), bf16),
            pltpu.VMEM((4, 1, 512), f32),
            pltpu.VMEM((NZ, NX, 64, 1024), bf16),
            pltpu.VMEM((2, WAVES, 2, NX, 64, n), bf16),
            pltpu.VMEM((2, 1024, n), bf16),
            pltpu.VMEM((2, 2, NZ, NX, 64, n), f32),
            pltpu.VMEM((2, 2, NZ, 2, 32, n), f32),
            pltpu.VMEM((WAVES, 2, NZ // 2, NX, 64, n), bf16),
            pltpu.VMEM((WAVES, 2, NZ // 2, NX, 64, n), bf16),
            pltpu.VMEM((WAVES, 2, NX // 2, NZ, 64, n), bf16),
            pltpu.VMEM((WAVES, 2, NX // 2, NZ, 64, n), bf16),
            pltpu.VMEM((WAVES, 2, NX // 2, 2, 32, n), bf16),
            pltpu.VMEM((WAVES, 2, NX // 2, 2, 32, n), bf16),
            pltpu.VMEM((WAVES, 2, NZ // 2, 2, 32, n), bf16),
            pltpu.VMEM((WAVES, 2, NZ // 2, 2, 32, n), bf16),
            dma((WAVES,)),
            dma((WAVES, NX)),
            dma((2, WAVES)),
            dma((2, WAVES, 3)),
            dma((WAVES, 2, NZ // 2)),
            dma((WAVES, 2, NZ // 2)),
            dma((WAVES, 2, NX // 2)),
            dma((WAVES, 2, NX // 2)),
            dma((WAVES, 2, NX // 2)),
            dma((WAVES, 2, NX // 2)),
            dma((WAVES, 2, NZ // 2)),
            dma((WAVES, 2, NZ // 2)),
        ],
        compiler_params=pltpu.CompilerParams(
            collective_id=0, has_side_effects=True, vmem_limit_bytes=56 * 2**20
        ),
    )(raw_blocks.reshape(2, NZ, NX, 64, 512), occupancy, exponent)


def solution(mesh):
    placed = (P(None, "row", "col"), P("row", "col"), P("row", "col"))
    return jax.shard_map(
        on_device,
        mesh=mesh,
        in_specs=placed,
        out_specs=P(None, None, ("row", "col"), None),
        check_vma=False,
    )
```

```python
import functools

import jax
import jax.numpy as jnp
from jax import lax
from jax.experimental import pallas as pl
from jax.experimental.pallas import tpu as pltpu
from jax.sharding import PartitionSpec as P

MESH = pl.DeviceIdType.MESH
NY, NZ, NX = 4, 8, 4
WAVES = 4
LANES = 128
SPAN = 2
FAR = 6


def wrap(index, size):
    return lax.rem(index + size, size)


class Chain:
    def __init__(self, n, me, neighbour, own, groups, send, recv, send_sem, recv_sem):
        self.n, self.me, self.neighbour, self.own, self.groups = n, me, neighbour, own, groups
        self.send, self.recv, self.send_sem, self.recv_sem = send, recv, send_sem, recv_sem
        self.started = []

    def half(self, side):
        size = self.groups // 2
        return pl.ds(size * side, size)

    def copy(self, side, step):
        if step == 0:
            cut = self.half(side)
            source, target = self.send.at[side, 0, cut], self.recv.at[side, 0, cut]
        else:
            source, target = self.send.at[side, step], self.recv.at[side, step]
        return pltpu.make_async_remote_copy(
            src_ref=source,
            dst_ref=target,
            send_sem=self.send_sem.at[side, step],
            recv_sem=self.recv_sem.at[side, step],
            device_id=self.neighbour(1 - 2 * side),
            device_id_type=MESH,
        )

    def step(self, step):
        for side in range(2):
            away = self.n // 2 - step
            dest = wrap(self.me + (1 - 2 * side) * away, self.n)
            size = self.groups // 2
            halves = (side, 1 - side) if step else (side,)
            if step:
                self.copy(side, step - 1).wait_recv()
            for part in halves:
                with_received = step > 1 or (step == 1 and part == side)

                def block(g, _, part=part, with_received=with_received, dest=dest, side=side):
                    at = part * size + g
                    value = self.own(dest, at)
                    if with_received:
                        value = value + self.recv[side, step - 1, at].astype(jnp.float32)
                    self.send[side, step, at] = value.astype(jnp.bfloat16)
                    return _

                lax.fori_loop(0, size, block, 0)
            copy = self.copy(side, step)
            copy.start()
            self.started.append(copy)

    def finish(self, put):
        last = self.n // 2 - 1
        for side in range(2):
            self.copy(side, last).wait_recv()

        def block(g, _):
            value = self.own(self.me, g)
            for side in range(2):
                value = value + self.recv[side, last, g].astype(jnp.float32)
            put(g, value)
            return _

        lax.fori_loop(0, self.groups, block, 0)

    def drain(self):
        for copy in self.started:
            copy.wait_send()


def kernel(
    raw_ref, occ_ref, exp_ref, out_ref,
    raw, factor, mine, land, hold, rhs, part, summed,
    z_send, z_recv, x_send, x_recv, zx_send, zx_recv, xz_send, xz_recv,
    raw_sem, root_sem, land_sem, hold_sem, relay_sem, pass_sem,
    z_ss, z_rs, x_ss, x_rs, zx_ss, zx_rs, xz_ss, xz_rs,
):
    row, col = lax.axis_index("row"), lax.axis_index("col")
    y, core, z, x = row // 2, row % 2, col // NX, col % NX

    def device(y, core, z, x):
        return (wrap(y, NY) * 2 + core, wrap(z, NZ) * NX + wrap(x, NX))

    def along_z(step):
        return device(y, core, z + step, x)

    def along_x(step):
        return device(y, core, z, x + step)

    def along_y(step):
        return device(y + step, core, z, x)

    other = device(y, 1 - core, z, x)
    fetches = [
        pltpu.make_async_copy(
            raw_ref.at[:, :, :, :, pl.ds(LANES * q, LANES)],
            raw.at[:, :, :, :, pl.ds(LANES * q, LANES)],
            raw_sem.at[q],
        )
        for q in range(WAVES)
    ]
    for fetch in fetches:
        fetch.start()

    barrier = pltpu.get_barrier_semaphore()
    for peer in (along_z(1), along_z(-1), along_x(1), along_x(-1), along_y(1), along_y(-1), other):
        pl.semaphore_signal(barrier, inc=1, device_id=peer, device_id_type=MESH)
    expected = jnp.int32(7)
    both = jnp.logical_and
    root_col = [p * (NZ * NX // 2) for p in range(2)]
    is_root = [col == c for c in root_col]
    odd = x % 2 == 1

    def distance(p, plane):
        return wrap(plane - p * (NZ // 2), NZ)

    def moved(p, plane):
        d = distance(p, plane)
        return jnp.logical_or(jnp.logical_or(d == 3, d == 4), d == 7)

    prior = wrap(row - 2, NZ)
    here = [distance(p, row) == 0 for p in range(2)]
    direct = [both(is_root[p], jnp.logical_not(moved(p, row))) for p in range(2)]
    relay_x = [
        both(jnp.logical_or(col == root_col[p] + 1, col == root_col[p] + 3), jnp.logical_not(here[p]))
        for p in range(2)
    ]
    relay_n = [both(col == root_col[p] + 3, here[p]) for p in range(2)]
    relay_y = [both(is_root[p], moved(p, prior)) for p in range(2)]
    match = core == z % 2
    dy = [wrap(y - z // 2 - both(jnp.logical_not(odd), moved(p, z)).astype(jnp.int32), NY) for p in range(2)]
    first = [both(match, dy[p] == 0) for p in range(2)]

    greet = []
    for p in range(2):
        greet.append((both(direct[p], jnp.logical_not(here[p])), row * NX))
        greet.append((direct[p], row * NX + 2))
        greet.append((relay_x[p], row * NX + x))
        greet.append((relay_y[p], prior * NX))
        greet.append((relay_y[p], prior * NX + 2))
        near = both(distance(p, z) == 0, x != 2)
        greet.append((both(first[p], jnp.logical_not(near)), root_col[p] + jnp.where(odd, x, 0)))
    for needed, peer in greet:
        expected = expected + needed.astype(jnp.int32)

        @pl.when(needed)
        def _(peer=peer):
            pl.semaphore_signal(barrier, inc=1, device_id=(row, peer), device_id_type=MESH)

    present = occ_ref[...].astype(jnp.float32)
    for tile in range(NZ // 2):
        exponent = exp_ref[tile, 0]
        scale = jnp.float32(1.0)
        for power in (-2, -1, 1, 2):
            scale = jnp.where(exponent == power, jnp.float32(2.0**power), scale)
        factor[tile] = present[tile : tile + 1] * scale

    def piece(j, q, h):
        return mine.at[2 * j + h, :, :, pl.ds(2 * LANES * q, 2 * LANES)]

    def give(source, target, send_sem, recv_sem, peer):
        return pltpu.make_async_remote_copy(
            src_ref=source, dst_ref=target, send_sem=send_sem, recv_sem=recv_sem,
            device_id=peer, device_id_type=MESH,
        )

    def root_copies(p, q, h):
        def to(j, target, recv_sem, peer):
            return give(piece(j, q, h), target, root_sem.at[q, h, j], recv_sem, peer)

        held = hold.at[0, q, h], hold_sem.at[0, q, h]
        held_too = hold.at[1, q, h], hold_sem.at[1, q, h]
        landed = land.at[p, 2 * q + h], land_sem.at[p, 2 * q + h]
        far = both(is_root[p], jnp.logical_not(here[p]))
        close = both(is_root[p], here[p])
        for j in (1, 3):
            peer = (row, jnp.int32(root_col[p] + j))
            yield far, to(j, *held, peer)
            yield close, to(j, *landed, peer)
        shift = both(is_root[p], moved(p, row))
        yield both(direct[p], jnp.logical_not(here[p])), to(0, *landed, (row, row * NX))
        yield shift, to(0, *held, along_y(1))
        yield both(direct[p], jnp.logical_not(here[p])), to(2, *landed, (row, row * NX + 2))
        if h == 0:
            yield close, to(2, *landed, (row, row * NX + 2))
        else:
            yield close, to(2, *held_too, (row, jnp.int32(root_col[p] + 3)))
        yield shift, to(2, *held_too, along_y(1))

    def relay_copies(p, q, h):
        for needed, slot, target in (
            (relay_x[p], 0, row * NX + x),
            (relay_y[p], 0, prior * NX),
            (relay_y[p], 1, prior * NX + 2),
            (relay_n[p], 1, row * NX + 2),
        ):
            if needed is relay_n[p] and h == 0:
                continue
            kind = 1 if needed is relay_y[p] else 0
            yield needed, slot, give(
                hold.at[slot, q, h], land.at[p, 2 * q + h], relay_sem.at[kind, slot, q, h], land_sem.at[p, 2 * q + h],
                (row, target),
            )

    def stay_copy(p, q, h):
        return pltpu.make_async_copy(piece(0, q, h), land.at[p, 2 * q + h], land_sem.at[p, 2 * q + h])

    for q in range(WAVES):
        fetches[q].wait()

        def decode(zd, _, q=q):
            f = factor[zd // 2, :, LANES * q : LANES * (q + 1)]
            for half in range(2):
                value = raw[half, zd, :, :, LANES * q : LANES * (q + 1)].astype(jnp.float32)
                start = 2 * LANES * q + LANES * half
                mine[zd, :, :, start : start + LANES] = (value * f[None]).astype(jnp.bfloat16)
            return _

        lax.fori_loop(0, NZ, decode, 0)
        if q == 0:
            pl.semaphore_wait(barrier, expected)
        for p in range(2):
            for h in range(2):
                for needed, copy in root_copies(p, q, h):

                    @pl.when(needed)
                    def _(copy=copy):
                        copy.start()

                @pl.when(both(is_root[p], here[p]))
                def _(p=p, q=q, h=h):
                    stay_copy(p, q, h).start()

    def relay(q, h):
        for p in range(2):
            for needed, slot, copy in relay_copies(p, q, h):

                @pl.when(needed)
                def _(copy=copy, slot=slot):
                    pltpu.make_async_copy(hold.at[slot, q, h], hold.at[slot, q, h], hold_sem.at[slot, q, h]).wait()
                    copy.start()

    def passes(p, i):
        onward, last = (1, NY - 1) if p == 0 else (-1, 1)
        for slot, (needed, peer) in enumerate(((dy[p] != last, along_y(onward)), (dy[p] >= 0, other))):
            copy = give(land.at[p, i], land.at[p, i], pass_sem.at[p, i, slot], land_sem.at[p, i], peer)
            yield both(match, needed), copy

    def hops(p):
        even = jnp.where(distance(p, z) == 0, jnp.where(x == 0, 0, 2), jnp.where(moved(p, z), 2, 1))
        at_first = jnp.where(odd, jnp.where(distance(p, z) == 0, 1, 2), even)
        return at_first + (dy[p] if p == 0 else wrap(-dy[p], NY)) + 1 - match.astype(jnp.int32)

    away = [hops(p) for p in range(2)]

    def arrive(p, tick):
        i = tick - away[p]

        @pl.when(both(i >= 0, i < 2 * WAVES))
        def _():
            pltpu.make_async_copy(land.at[p, i], land.at[p, i], land_sem.at[p, i]).wait()
            for needed, copy in passes(p, i):

                @pl.when(needed)
                def _(copy=copy):
                    copy.start()

    def build(p, q):
        for k in range(4):
            block = land[p, 2 * q + k // 2, 2 * (k % 2) : 2 * (k % 2) + 2].reshape(LANES, 2 * LANES)
            real, imag = block[:, :LANES], block[:, LANES:]
            at = 2 * LANES * k
            rhs[p, at : at + LANES, :] = block
            rhs[p, at + LANES : at + 2 * LANES, :LANES] = -imag
            rhs[p, at + LANES : at + 2 * LANES, LANES:] = real

    def product(p, rows):
        return jnp.dot(rows.reshape(8 * 64, 8 * LANES), rhs[p], preferred_element_type=jnp.float32)

    def multiply_z(slot, start, count):
        def block(k, _):
            pair = [wrap(z + NZ // 2 + 2 * k + i, NZ) for i in range(2)]
            rows = jnp.concatenate([mine[zd] for zd in pair], axis=0)
            terms = product(0, rows).reshape(2, 4, 64, 2 * LANES)
            for i, zd in enumerate(pair):
                part[slot, 0, zd] = terms[i]
            return _

        lax.fori_loop(start, start + count, block, 0)

    def multiply_x(slot, start, count):
        def block(k, _):
            xd = wrap(x + NX // 2 + k, NX)
            part[slot, 1, :, xd] = product(1, mine[:, xd]).reshape(8, 64, 2 * LANES)
            return _

        lax.fori_loop(start, start + count, block, 0)

    def chains(w):
        slot = w
        first_z = Chain(
            NZ, z, along_z, lambda d, g: part[slot, 0, d, g], NX,
            z_send.at[w], z_recv.at[w], z_ss.at[w], z_rs.at[w],
        )
        first_x = Chain(
            NX, x, along_x, lambda d, g: part[slot, 1, g, d], NZ,
            x_send.at[w], x_recv.at[w], x_ss.at[w], x_rs.at[w],
        )
        then_x = Chain(
            NX, x, along_x, lambda d, g: summed[slot, 0, d, g], 2,
            zx_send.at[w], zx_recv.at[w], zx_ss.at[w], zx_rs.at[w],
        )
        then_z = Chain(
            NZ, z, along_z, lambda d, g: summed[slot, 1, d, g], 2,
            xz_send.at[w], xz_recv.at[w], xz_ss.at[w], xz_rs.at[w],
        )
        return first_z, first_x, then_x, then_z

    all_chains = [chains(w) for w in range(WAVES)]

    def keep(slot, which):
        def put(g, value):
            summed[slot, which, g] = value.reshape(2, 32, 2 * LANES)

        return put

    def result(p, w):
        def put(g, value):
            value = value.astype(jnp.bfloat16)
            for half in range(2):
                out_ref[p, half, pl.ds(pl.multiple_of(32 * g, 32), 32), LANES * w : LANES * (w + 1)] = value[
                    :, LANES * half : LANES * (half + 1)
                ]

        return put

    def heads(w):
        first_z, first_x, _, _ = all_chains[w]
        build(0, w)
        multiply_z(w, 0, 1)
        first_z.step(0)
        build(1, w)
        multiply_x(w, 0, 1)
        first_x.step(0)

    def rest(w):
        multiply_z(w, 1, 3)
        multiply_x(w, 1, 3)

    def run(w, k):
        first_z, first_x, then_x, then_z = all_chains[w]
        slot = w
        if 1 <= k <= 3:
            first_z.step(k)
        if k == 1:
            first_x.step(1)
        if k == 2:
            first_x.finish(keep(slot, 1))
        if 2 <= k <= 5:
            then_z.step(k - 2)
        if k == 4:
            first_z.finish(keep(slot, 0))
        if 4 <= k <= 5:
            then_x.step(k - 4)
        if k == 6:
            then_x.finish(result(0, w))
            then_z.finish(result(1, w))

    for tick in range(FAR + SPAN * (WAVES - 1) + 8):
        if 1 <= tick <= 2 * WAVES:
            relay((tick - 1) // 2, (tick - 1) % 2)
        if tick < 2 * WAVES + FAR:
            for p in range(2):
                arrive(p, tick)
        for w in range(WAVES):
            k = tick - FAR - 1 - SPAN * w
            if k == 0:
                heads(w)
            if 1 <= k <= 6:
                run(w, k)
            if k == 0:
                rest(w)

    for group in all_chains:
        for chain in group:
            chain.drain()
    for p in range(2):
        for q in range(WAVES):
            for h in range(2):
                sent = [*root_copies(p, q, h), *passes(p, 2 * q + h)]
                sent += [(needed, copy) for needed, _, copy in relay_copies(p, q, h)]
                for needed, copy in sent:

                    @pl.when(needed)
                    def _(copy=copy):
                        copy.wait_send()


def on_device(raw_blocks, occupancy, exponent):
    bf16, f32 = jnp.bfloat16, jnp.float32
    dma = pltpu.SemaphoreType.DMA
    n = 2 * LANES
    return pl.pallas_call(
        kernel,
        out_shape=jax.ShapeDtypeStruct((2, 2, 64, 512), bf16),
        in_specs=[
            pl.BlockSpec(memory_space=pl.ANY),
            pl.BlockSpec(memory_space=pltpu.VMEM),
            pl.BlockSpec(memory_space=pltpu.SMEM),
        ],
        out_specs=pl.BlockSpec(memory_space=pltpu.VMEM),
        scratch_shapes=[
            pltpu.VMEM((2, NZ, NX, 64, 512), bf16),
            pltpu.VMEM((4, 1, 512), f32),
            pltpu.VMEM((NZ, NX, 64, 1024), bf16),
            pltpu.VMEM((2, 2 * WAVES, NX, 64, n), bf16),
            pltpu.VMEM((2, WAVES, 2, NX, 64, n), bf16),
            pltpu.VMEM((2, 1024, n), bf16),
            pltpu.VMEM((WAVES, 2, NZ, NX, 64, n), f32),
            pltpu.VMEM((WAVES, 2, NZ, 2, 32, n), f32),
            pltpu.VMEM((WAVES, 2, NZ // 2, NX, 64, n), bf16),
            pltpu.VMEM((WAVES, 2, NZ // 2, NX, 64, n), bf16),
            pltpu.VMEM((WAVES, 2, NX // 2, NZ, 64, n), bf16),
            pltpu.VMEM((WAVES, 2, NX // 2, NZ, 64, n), bf16),
            pltpu.VMEM((WAVES, 2, NX // 2, 2, 32, n), bf16),
            pltpu.VMEM((WAVES, 2, NX // 2, 2, 32, n), bf16),
            pltpu.VMEM((WAVES, 2, NZ // 2, 2, 32, n), bf16),
            pltpu.VMEM((WAVES, 2, NZ // 2, 2, 32, n), bf16),
            dma((WAVES,)),
            dma((WAVES, 2, NX)),
            dma((2, 2 * WAVES)),
            dma((2, WAVES, 2)),
            dma((2, 2, WAVES, 2)),
            dma((2, 2 * WAVES, 2)),
            dma((WAVES, 2, NZ // 2)),
            dma((WAVES, 2, NZ // 2)),
            dma((WAVES, 2, NX // 2)),
            dma((WAVES, 2, NX // 2)),
            dma((WAVES, 2, NX // 2)),
            dma((WAVES, 2, NX // 2)),
            dma((WAVES, 2, NZ // 2)),
            dma((WAVES, 2, NZ // 2)),
        ],
        compiler_params=pltpu.CompilerParams(
            collective_id=0, has_side_effects=True, vmem_limit_bytes=60 * 2**20
        ),
    )(raw_blocks.reshape(2, NZ, NX, 64, 512), occupancy, exponent)


def solution(mesh):
    placed = (P(None, "row", "col"), P("row", "col"), P("row", "col"))
    return jax.shard_map(
        on_device,
        mesh=mesh,
        in_specs=placed,
        out_specs=P(None, None, ("row", "col"), None),
        check_vma=False,
    )
```

```python
import functools

import jax
import jax.numpy as jnp
from jax import lax
from jax.experimental import pallas as pl
from jax.experimental.pallas import tpu as pltpu
from jax.sharding import PartitionSpec as P

MESH = pl.DeviceIdType.MESH
NY, NZ, NX = 4, 8, 4
WAVES = 4
LANES = 128
PACE = 2
HOP = 3
DEEP = 2
ORDER = (
    "k0", "k1", "k2", "k3", "k4", "k5", "k6", "k7", "k8", "k9", "k10", "k11", "k12", "k13", "k14", "k15",
    "k16", "k17", "0H", "0M", "k18", "1H", "1M", "k19", "k20", "0s1", "k21", "3H", "2H", "2M", "k22", "3M",
    "k23", "0s2", "k24", "1s1", "2s1", "k25", "3s1", "4H", "4M", "k26", "5H", "k27", "5M", "k28", "0s3", "k29",
    "7H", "6H", "2s2", "6M", "4s1", "1f", "7M", "0f", "6s1", "3f", "2s3", "5s1", "4s2", "1t1", "7s1", "0t1",
    "6s2", "3t1", "2f", "5f", "4s3", "1t2", "7f", "6s3", "0F", "2t1", "3t2", "5t1", "2F", "4f", "1t3", "7t1",
    "4t1", "6f", "3t3", "5t2", "4F", "1F", "7t2", "6t1", "3F", "5t3", "7t3", "6F", "5F", "7F",
)


def wrap(index, size):
    return lax.rem(index + size, size)


class Chain:
    def __init__(self, n, me, neighbour, own, groups, send, recv, send_sem, recv_sem):
        self.n, self.me, self.neighbour, self.own, self.groups = n, me, neighbour, own, groups
        self.send, self.recv, self.send_sem, self.recv_sem = send, recv, send_sem, recv_sem
        self.started = []

    def half(self, side):
        size = self.groups // 2
        return pl.ds(size * side, size)

    def copy(self, side, step):
        if step == 0:
            cut = self.half(side)
            source, target = self.send.at[side, 0, cut], self.recv.at[side, 0, cut]
        else:
            source, target = self.send.at[side, step], self.recv.at[side, step]
        return pltpu.make_async_remote_copy(
            src_ref=source,
            dst_ref=target,
            send_sem=self.send_sem.at[side, step],
            recv_sem=self.recv_sem.at[side, step],
            device_id=self.neighbour(1 - 2 * side),
            device_id_type=MESH,
        )

    def step(self, step):
        for side in range(2):
            away = self.n // 2 - step
            dest = wrap(self.me + (1 - 2 * side) * away, self.n)
            size = self.groups // 2
            halves = (side, 1 - side) if step else (side,)
            if step:
                self.copy(side, step - 1).wait_recv()
            for part in halves:
                with_received = step > 1 or (step == 1 and part == side)

                def block(g, _, part=part, with_received=with_received, dest=dest, side=side):
                    at = part * size + g
                    value = self.own(dest, at)
                    if with_received:
                        value = value + self.recv[side, step - 1, at].astype(jnp.float32)
                    self.send[side, step, at] = value.astype(jnp.bfloat16)
                    return _

                lax.fori_loop(0, size, block, 0)
            copy = self.copy(side, step)
            copy.start()
            self.started.append(copy)

    def finish(self, put):
        last = self.n // 2 - 1
        for side in range(2):
            self.copy(side, last).wait_recv()

        def block(g, _):
            value = self.own(self.me, g)
            for side in range(2):
                value = value + self.recv[side, last, g].astype(jnp.float32)
            put(g, value)
            return _

        lax.fori_loop(0, self.groups, block, 0)

    def drain(self):
        for copy in self.started:
            copy.wait_send()


def kernel(
    raw_ref, occ_ref, exp_ref, out_ref,
    raw, factor, mine, land, hold, rhs, part, summed,
    z_send, z_recv, x_send, x_recv, zx_send, zx_recv, xz_send, xz_recv,
    raw_sem, root_sem, land_sem, hold_sem, relay_sem, pass_sem,
    z_ss, z_rs, x_ss, x_rs, zx_ss, zx_rs, xz_ss, xz_rs,
):
    row, col = lax.axis_index("row"), lax.axis_index("col")
    y, core, z, x = row // 2, row % 2, col // NX, col % NX

    def device(y, core, z, x):
        return (wrap(y, NY) * 2 + core, wrap(z, NZ) * NX + wrap(x, NX))

    def along_z(step):
        return device(y, core, z + step, x)

    def along_x(step):
        return device(y, core, z, x + step)

    def along_y(step):
        return device(y + step, core, z, x)

    other = device(y, 1 - core, z, x)
    fetches = [
        pltpu.make_async_copy(
            raw_ref.at[:, :, :, :, pl.ds(LANES * q, LANES)],
            raw.at[:, :, :, :, pl.ds(LANES * q, LANES)],
            raw_sem.at[q],
        )
        for q in range(WAVES)
    ]
    for fetch in fetches:
        fetch.start()

    barrier = pltpu.get_barrier_semaphore()
    for peer in (along_z(1), along_z(-1), along_x(1), along_x(-1), along_y(1), along_y(-1), other):
        pl.semaphore_signal(barrier, inc=1, device_id=peer, device_id_type=MESH)
    expected = jnp.int32(7)
    both = jnp.logical_and
    root_col = [p * (NZ * NX // 2) for p in range(2)]
    is_root = [col == c for c in root_col]
    odd = x % 2 == 1

    def distance(p, plane):
        return wrap(plane - p * (NZ // 2), NZ)

    def moved(p, plane):
        d = distance(p, plane)
        return jnp.logical_or(jnp.logical_or(d == 3, d == 4), d == 7)

    prior = wrap(row - 2, NZ)
    here = [distance(p, row) == 0 for p in range(2)]
    direct = [both(is_root[p], jnp.logical_not(moved(p, row))) for p in range(2)]
    relay_x = [
        both(jnp.logical_or(col == root_col[p] + 1, col == root_col[p] + 3), jnp.logical_not(here[p]))
        for p in range(2)
    ]
    relay_n = [both(col == root_col[p] + 3, here[p]) for p in range(2)]
    relay_y = [both(is_root[p], moved(p, prior)) for p in range(2)]
    match = core == z % 2
    dy = [wrap(y - z // 2 - both(jnp.logical_not(odd), moved(p, z)).astype(jnp.int32), NY) for p in range(2)]
    first = [both(match, dy[p] == 0) for p in range(2)]

    greet = []
    for p in range(2):
        greet.append((both(direct[p], jnp.logical_not(here[p])), row * NX))
        greet.append((direct[p], row * NX + 2))
        greet.append((relay_x[p], row * NX + x))
        greet.append((relay_y[p], prior * NX))
        greet.append((relay_y[p], prior * NX + 2))
        near = both(distance(p, z) == 0, x != 2)
        greet.append((both(first[p], jnp.logical_not(near)), root_col[p] + jnp.where(odd, x, 0)))
    for needed, peer in greet:
        expected = expected + needed.astype(jnp.int32)

        @pl.when(needed)
        def _(peer=peer):
            pl.semaphore_signal(barrier, inc=1, device_id=(row, peer), device_id_type=MESH)

    present = occ_ref[...].astype(jnp.float32)
    for tile in range(NZ // 2):
        exponent = exp_ref[tile, 0]
        scale = jnp.float32(1.0)
        for power in (-2, -1, 1, 2):
            scale = jnp.where(exponent == power, jnp.float32(2.0**power), scale)
        factor[tile] = present[tile : tile + 1] * scale

    def piece(j, q, h):
        return mine.at[2 * j + h, :, :, pl.ds(2 * LANES * q, 2 * LANES)]

    def give(source, target, send_sem, recv_sem, peer):
        return pltpu.make_async_remote_copy(
            src_ref=source, dst_ref=target, send_sem=send_sem, recv_sem=recv_sem,
            device_id=peer, device_id_type=MESH,
        )

    def root_copies(p, q, h):
        def to(j, target, recv_sem, peer):
            return give(piece(j, q, h), target, root_sem.at[q, h, j], recv_sem, peer)

        held = hold.at[0, q, h], hold_sem.at[0, q, h]
        held_too = hold.at[1, q, h], hold_sem.at[1, q, h]
        landed = land.at[p, 2 * q + h], land_sem.at[p, 2 * q + h]
        far = both(is_root[p], jnp.logical_not(here[p]))
        close = both(is_root[p], here[p])
        for j in (1, 3):
            peer = (row, jnp.int32(root_col[p] + j))
            yield far, to(j, *held, peer)
            yield close, to(j, *landed, peer)
        shift = both(is_root[p], moved(p, row))
        yield both(direct[p], jnp.logical_not(here[p])), to(0, *landed, (row, row * NX))
        yield shift, to(0, *held, along_y(1))
        yield both(direct[p], jnp.logical_not(here[p])), to(2, *landed, (row, row * NX + 2))
        if h == 0:
            yield close, to(2, *landed, (row, row * NX + 2))
        else:
            yield close, to(2, *held_too, (row, jnp.int32(root_col[p] + 3)))
        yield shift, to(2, *held_too, along_y(1))

    def relay_copies(p, q, h):
        for needed, slot, target in (
            (relay_x[p], 0, row * NX + x),
            (relay_y[p], 0, prior * NX),
            (relay_y[p], 1, prior * NX + 2),
            (relay_n[p], 1, row * NX + 2),
        ):
            if needed is relay_n[p] and h == 0:
                continue
            kind = 1 if needed is relay_y[p] else 0
            yield needed, slot, give(
                hold.at[slot, q, h], land.at[p, 2 * q + h], relay_sem.at[kind, slot, q, h], land_sem.at[p, 2 * q + h],
                (row, target),
            )

    def stay_copy(p, q, h):
        return pltpu.make_async_copy(piece(0, q, h), land.at[p, 2 * q + h], land_sem.at[p, 2 * q + h])

    def emit(i):
        for p in range(2):
            if i >= DEEP:
                for needed, copy in root_copies(p, (i - DEEP) // 2, (i - DEEP) % 2):

                    @pl.when(needed)
                    def _(copy=copy):
                        copy.wait_send()

            for needed, copy in root_copies(p, i // 2, i % 2):

                @pl.when(needed)
                def _(copy=copy):
                    copy.start()

            @pl.when(both(is_root[p], here[p]))
            def _(p=p):
                stay_copy(p, i // 2, i % 2).start()

    for q in range(WAVES):
        fetches[q].wait()

        def decode(zd, _, q=q):
            f = factor[zd // 2, :, LANES * q : LANES * (q + 1)]
            for half in range(2):
                value = raw[half, zd, :, :, LANES * q : LANES * (q + 1)].astype(jnp.float32)
                start = 2 * LANES * q + LANES * half
                mine[zd, :, :, start : start + LANES] = (value * f[None]).astype(jnp.bfloat16)
            return _

        lax.fori_loop(0, NZ, decode, 0)
        if q == 0:
            pl.semaphore_wait(barrier, expected)
            emit(0)
            emit(1)

    def relay(q, h):
        for p in range(2):
            for needed, slot, copy in relay_copies(p, q, h):

                @pl.when(needed)
                def _(copy=copy, slot=slot):
                    pltpu.make_async_copy(hold.at[slot, q, h], hold.at[slot, q, h], hold_sem.at[slot, q, h]).wait()
                    copy.start()

    busy = [both(x == 0, distance(p, z) == 0) for p in range(2)]

    def passes(p, i):
        pull = i % 2
        up = both(jnp.logical_not(busy[p]), jnp.logical_or(dy[p] == 0, both(dy[p] == 1, pull == 0)))
        down = jnp.logical_or(dy[p] == 0, both(dy[p] == NY - 1, pull == 1))
        down = jnp.where(busy[p], dy[p] != 1, down)
        for slot, (needed, peer) in enumerate(((up, along_y(1)), (down, along_y(-1)), (dy[p] >= 0, other))):
            copy = give(land.at[p, i], land.at[p, i], pass_sem.at[p, i, slot], land_sem.at[p, i], peer)
            yield both(match, needed), copy

    def hops(p):
        even = jnp.where(distance(p, z) == 0, jnp.where(x == 0, 0, 2), jnp.where(moved(p, z), 2, 1))
        at_first = jnp.where(odd, jnp.where(distance(p, z) == 0, 1, 2), even)
        return at_first + jnp.where(both(dy[p] == 1, jnp.logical_not(busy[p])), 1, wrap(-dy[p], NY)) + 1 - match.astype(jnp.int32)

    away = [hops(p) for p in range(2)]

    def arrive(p, tick):
        late = tick - HOP * away[p]
        i = late // PACE

        @pl.when(both(both(late >= 0, late % PACE == 0), i < 2 * WAVES))
        def _():
            pltpu.make_async_copy(land.at[p, i], land.at[p, i], land_sem.at[p, i]).wait()
            for needed, copy in passes(p, i):

                @pl.when(needed)
                def _(copy=copy):
                    copy.start()

    def build(p, q):
        for k in range(4):
            block = land[p, 2 * q + k // 2, 2 * (k % 2) : 2 * (k % 2) + 2].reshape(LANES, 2 * LANES)
            real, imag = block[:, :LANES], block[:, LANES:]
            at = 2 * LANES * k
            rhs[q, p, at : at + LANES, :] = block
            rhs[q, p, at + LANES : at + 2 * LANES, :LANES] = -imag
            rhs[q, p, at + LANES : at + 2 * LANES, LANES:] = real

    def product(w, p, rows):
        return jnp.dot(rows.reshape(8 * 64, 8 * LANES), rhs[w, p], preferred_element_type=jnp.float32)

    def multiply_z(slot, start, count):
        def block(k, _):
            pair = [wrap(z + NZ // 2 + 2 * k + i, NZ) for i in range(2)]
            rows = jnp.concatenate([mine[zd] for zd in pair], axis=0)
            terms = product(slot, 0, rows).reshape(2, 4, 64, 2 * LANES)
            for i, zd in enumerate(pair):
                part[slot, 0, zd] = terms[i]
            return _

        lax.fori_loop(start, start + count, block, 0)

    def multiply_x(slot, start, count):
        def block(k, _):
            xd = wrap(x + NX // 2 + k, NX)
            part[slot, 1, :, xd] = product(slot, 1, mine[:, xd]).reshape(8, 64, 2 * LANES)
            return _

        lax.fori_loop(start, start + count, block, 0)

    def chains(w):
        slot = w
        first_z = Chain(
            NZ, z, along_z, lambda d, g: part[slot, 0, d, g], NX,
            z_send.at[w], z_recv.at[w], z_ss.at[w], z_rs.at[w],
        )
        first_x = Chain(
            NX, x, along_x, lambda d, g: part[slot, 1, g, d], NZ,
            x_send.at[w], x_recv.at[w], x_ss.at[w], x_rs.at[w],
        )
        then_x = Chain(
            NX, x, along_x, lambda d, g: summed[slot, 0, d, g], 2,
            zx_send.at[w], zx_recv.at[w], zx_ss.at[w], zx_rs.at[w],
        )
        then_z = Chain(
            NZ, z, along_z, lambda d, g: summed[slot, 1, d, g], 2,
            xz_send.at[w], xz_recv.at[w], xz_ss.at[w], xz_rs.at[w],
        )
        return first_z, first_x, then_x, then_z

    all_chains = [chains(w) for w in range(WAVES)]

    def keep(slot, which):
        def put(g, value):
            summed[slot, which, g] = value.reshape(2, 32, 2 * LANES)

        return put

    def result(p, w):
        def put(g, value):
            value = value.astype(jnp.bfloat16)
            for half in range(2):
                out_ref[p, half, pl.ds(pl.multiple_of(32 * g, 32), 32), LANES * w : LANES * (w + 1)] = value[
                    :, LANES * half : LANES * (half + 1)
                ]

        return put

    def run(group, op):
        w, which = group // 2, group % 2
        first, then = (all_chains[w][0], all_chains[w][2]) if which == 0 else (all_chains[w][1], all_chains[w][3])
        multiply = multiply_x if which else multiply_z
        if op == "H":
            build(which, w)
            multiply(w, 0, 1)
            first.step(0)
        elif op == "M":
            multiply(w, 1, 3)
        elif op == "f":
            first.finish(keep(w, which))
            then.step(0)
        elif op == "F":
            then.finish(result(which, w))
        else:
            (first if op[0] == "s" else then).step(int(op[1]))

    for token in ORDER:
        if token[0] == "k":
            tick = int(token[1:])
            if tick % PACE == 0 and 2 <= tick // PACE < 2 * WAVES:
                emit(tick // PACE)
            at = tick - HOP
            if at >= 0 and at % PACE == 0 and at // PACE < 2 * WAVES:
                relay(at // PACE // 2, at // PACE % 2)
            for p in range(2):
                arrive(p, tick)
        else:
            run(int(token[0]), token[1:])

    for group in all_chains:
        for chain in group:
            chain.drain()
    for p in range(2):
        for q in range(WAVES):
            for h in range(2):
                sent = [*passes(p, 2 * q + h)]
                if 2 * q + h >= 2 * WAVES - DEEP:
                    sent += root_copies(p, q, h)
                sent += [(needed, copy) for needed, _, copy in relay_copies(p, q, h)]
                for needed, copy in sent:

                    @pl.when(needed)
                    def _(copy=copy):
                        copy.wait_send()


def on_device(raw_blocks, occupancy, exponent):
    bf16, f32 = jnp.bfloat16, jnp.float32
    dma = pltpu.SemaphoreType.DMA
    n = 2 * LANES
    return pl.pallas_call(
        kernel,
        out_shape=jax.ShapeDtypeStruct((2, 2, 64, 512), bf16),
        in_specs=[
            pl.BlockSpec(memory_space=pl.ANY),
            pl.BlockSpec(memory_space=pltpu.VMEM),
            pl.BlockSpec(memory_space=pltpu.SMEM),
        ],
        out_specs=pl.BlockSpec(memory_space=pltpu.VMEM),
        scratch_shapes=[
            pltpu.VMEM((2, NZ, NX, 64, 512), bf16),
            pltpu.VMEM((4, 1, 512), f32),
            pltpu.VMEM((NZ, NX, 64, 1024), bf16),
            pltpu.VMEM((2, 2 * WAVES, NX, 64, n), bf16),
            pltpu.VMEM((2, WAVES, 2, NX, 64, n), bf16),
            pltpu.VMEM((WAVES, 2, 1024, n), bf16),
            pltpu.VMEM((WAVES, 2, NZ, NX, 64, n), f32),
            pltpu.VMEM((WAVES, 2, NZ, 2, 32, n), f32),
            pltpu.VMEM((WAVES, 2, NZ // 2, NX, 64, n), bf16),
            pltpu.VMEM((WAVES, 2, NZ // 2, NX, 64, n), bf16),
            pltpu.VMEM((WAVES, 2, NX // 2, NZ, 64, n), bf16),
            pltpu.VMEM((WAVES, 2, NX // 2, NZ, 64, n), bf16),
            pltpu.VMEM((WAVES, 2, NX // 2, 2, 32, n), bf16),
            pltpu.VMEM((WAVES, 2, NX // 2, 2, 32, n), bf16),
            pltpu.VMEM((WAVES, 2, NZ // 2, 2, 32, n), bf16),
            pltpu.VMEM((WAVES, 2, NZ // 2, 2, 32, n), bf16),
            dma((WAVES,)),
            dma((WAVES, 2, NX)),
            dma((2, 2 * WAVES)),
            dma((2, WAVES, 2)),
            dma((2, 2, WAVES, 2)),
            dma((2, 2 * WAVES, 3)),
            dma((WAVES, 2, NZ // 2)),
            dma((WAVES, 2, NZ // 2)),
            dma((WAVES, 2, NX // 2)),
            dma((WAVES, 2, NX // 2)),
            dma((WAVES, 2, NX // 2)),
            dma((WAVES, 2, NX // 2)),
            dma((WAVES, 2, NZ // 2)),
            dma((WAVES, 2, NZ // 2)),
        ],
        compiler_params=pltpu.CompilerParams(
            collective_id=0, has_side_effects=True, vmem_limit_bytes=60 * 2**20
        ),
    )(raw_blocks.reshape(2, NZ, NX, 64, 512), occupancy, exponent)


def solution(mesh):
    placed = (P(None, "row", "col"), P("row", "col"), P("row", "col"))
    return jax.shard_map(
        on_device,
        mesh=mesh,
        in_specs=placed,
        out_specs=P(None, None, ("row", "col"), None),
        check_vma=False,
    )
```

```python
import functools

import jax
import jax.numpy as jnp
from jax import lax
from jax.experimental import pallas as pl
from jax.experimental.pallas import tpu as pltpu
from jax.sharding import PartitionSpec as P

MESH = pl.DeviceIdType.MESH
NY, NZ, NX = 4, 8, 4
WAVES = 4
LANES = 128
PARTS = 4
ITEMS = PARTS * WAVES
PACE = 2
HOP = 5
DEEP = 4
EARLY = 99
KINDS = "ZXZXZXZX"
NUM_Z, NUM_X = KINDS.count("Z"), KINDS.count("X")
ORDER = (
    32, "0H", "0M", 34, "1H", "1M", 36, "0s1", 40, "2H", "1s1", 41, "2M", 42, "0s2", 43,
    "3H", "3M", 45, "2s1", 48, "4H", "4M", 50, "0s3", "1f", 51, "5H", "5M", 53, "2s2", "4s1",
    54, "3s1", 56, "7H", "6H", "0f", "5s1", "1t1", "6M", "7M", "2s3", "4s2", "3f", "6s1", "1t2", "7s1",
    "0t1", "2f", "4s3", "3t1", "5f", "6s2", "1t3", "4f", "7f", "3t2", "5t1", "0F", "2t1", "4t1", "6s3", "2F",
    "1F", "7t1", "3t3", "4F", "5t2", "6f", "7t2", "3F", "settle", "0drain", "1drain", "2drain", "3drain", "4drain", "5t3", "6t1",
    "7t3", "5F", "6F", "7F", "5drain", "6drain", "7drain",
)


def wrap(index, size):
    return lax.rem(index + size, size)


class Chain:
    def __init__(self, n, me, neighbour, own, groups, split, send, recv, send_sem, recv_sem):
        self.split = split
        self.n, self.me, self.neighbour, self.own, self.groups = n, me, neighbour, own, groups
        self.send, self.recv, self.send_sem, self.recv_sem = send, recv, send_sem, recv_sem
        self.started = []

    def half(self, side):
        size = self.groups // 2
        return pl.ds(size * side, size)

    def copy(self, side, step):
        if step == 0 or (self.split and step in (1, EARLY)):
            cut = self.half(1 - side if step == EARLY else side)
            at = min(step, 1)
            source, target = self.send.at[side, at, cut], self.recv.at[side, at, cut]
        else:
            source, target = self.send.at[side, step], self.recv.at[side, step]
        return pltpu.make_async_remote_copy(
            src_ref=source,
            dst_ref=target,
            send_sem=self.send_sem.at[side, min(step, self.n // 2)],
            recv_sem=self.recv_sem.at[side, min(step, self.n // 2)],
            device_id=self.neighbour(1 - 2 * side),
            device_id_type=MESH,
        )

    def landed(self, side, step):
        self.copy(side, step).wait_recv()
        if step == 1 and self.split:
            self.copy(side, EARLY).wait_recv()

    def step(self, step):
        for side in range(2):
            slot = min(step, 1) if step == EARLY else step
            away = self.n // 2 - slot
            dest = wrap(self.me + (1 - 2 * side) * away, self.n)
            size = self.groups // 2
            halves = (side, 1 - side) if step else (side,)
            if self.split and step == 1:
                halves = (side,)
            if step == EARLY:
                halves = (1 - side,)
            elif step:
                self.landed(side, step - 1)
            for part in halves:
                with_received = step != EARLY and (step > 1 or (step == 1 and part == side))

                def block(g, _, part=part, with_received=with_received, dest=dest, side=side, slot=slot):
                    at = part * size + g
                    value = self.own(dest, at)
                    if with_received:
                        value = value + self.recv[side, step - 1, at].astype(jnp.float32)
                    self.send[side, slot, at] = value.astype(jnp.bfloat16)
                    return _

                lax.fori_loop(0, size, block, 0)
            copy = self.copy(side, step)
            copy.start()
            self.started.append(copy)

    def finish(self, put):
        last = self.n // 2 - 1
        for side in range(2):
            self.landed(side, last)

        def block(g, _):
            value = self.own(self.me, g)
            for side in range(2):
                value = value + self.recv[side, last, g].astype(jnp.float32)
            put(g, value)
            return _

        lax.fori_loop(0, self.groups, block, 0)

    def drain(self):
        for copy in self.started:
            copy.wait_send()


def kernel(
    raw_ref, occ_ref, exp_ref, out_ref,
    power_of, power_sem, raw, factor, mine, land, hold, rhs, part, summed,
    z_send, z_recv, x_send, x_recv, zx_send, zx_recv, xz_send, xz_recv,
    raw_sem, root_sem, land_sem, hold_sem, relay_sem, pass_sem,
    z_ss, z_rs, x_ss, x_rs, zx_ss, zx_rs, xz_ss, xz_rs,
):
    row, col = lax.axis_index("row"), lax.axis_index("col")
    y, core, z, x = row // 2, row % 2, col // NX, col % NX

    def device(y, core, z, x):
        return (wrap(y, NY) * 2 + core, wrap(z, NZ) * NX + wrap(x, NX))

    def along_z(step):
        return device(y, core, z + step, x)

    def along_x(step):
        return device(y, core, z, x + step)

    def along_y(step):
        return device(y + step, core, z, x)

    other = device(y, 1 - core, z, x)
    fetches = [
        pltpu.make_async_copy(
            raw_ref.at[:, :, :, :, pl.ds(LANES * q, LANES)],
            raw.at[:, :, :, :, pl.ds(LANES * q, LANES)],
            raw_sem.at[q],
        )
        for q in range(WAVES)
    ]
    for fetch in fetches:
        fetch.start()

    barrier = pltpu.get_barrier_semaphore()
    for peer in (along_z(1), along_z(-1), along_x(1), along_x(-1), along_y(1), along_y(-1), other):
        pl.semaphore_signal(barrier, inc=1, device_id=peer, device_id_type=MESH)
    expected = jnp.int32(7)
    both = jnp.logical_and
    root_col = [p * (NZ * NX // 2) for p in range(2)]
    is_root = [col == c for c in root_col]
    odd = x % 2 == 1

    def distance(p, plane):
        return wrap(plane - p * (NZ // 2), NZ)

    def moved(p, plane):
        d = distance(p, plane)
        return jnp.logical_or(jnp.logical_or(d == 3, d == 4), d == 7)

    prior = wrap(row - 2, NZ)
    here = [distance(p, row) == 0 for p in range(2)]
    direct = [both(is_root[p], jnp.logical_not(moved(p, row))) for p in range(2)]
    relay_x = [
        both(jnp.logical_or(col == root_col[p] + 1, col == root_col[p] + 3), jnp.logical_not(here[p]))
        for p in range(2)
    ]
    relay_n = [both(col == root_col[p] + 3, here[p]) for p in range(2)]
    relay_y = [both(is_root[p], moved(p, prior)) for p in range(2)]
    match = core == z % 2
    dy = [wrap(y - z // 2 - both(jnp.logical_not(odd), moved(p, z)).astype(jnp.int32), NY) for p in range(2)]
    first = [both(match, dy[p] == 0) for p in range(2)]

    greet = []
    for p in range(2):
        greet.append((both(direct[p], jnp.logical_not(here[p])), row * NX))
        greet.append((direct[p], row * NX + 2))
        greet.append((relay_x[p], row * NX + x))
        greet.append((relay_y[p], prior * NX))
        greet.append((relay_y[p], prior * NX + 2))
        near = both(distance(p, z) == 0, x != 2)
        greet.append((both(first[p], jnp.logical_not(near)), root_col[p] + jnp.where(odd, x, 0)))
    for needed, peer in greet:
        expected = expected + needed.astype(jnp.int32)

        @pl.when(needed)
        def _(peer=peer):
            pl.semaphore_signal(barrier, inc=1, device_id=(row, peer), device_id_type=MESH)

    powers = pltpu.make_async_copy(exp_ref, power_of, power_sem)
    powers.start()
    powers.wait()
    present = occ_ref[...].astype(jnp.float32)
    for tile in range(NZ // 2):
        exponent = power_of[tile, 0]
        scale = jnp.float32(1.0)
        for power in (-2, -1, 1, 2):
            scale = jnp.where(exponent == power, jnp.float32(2.0**power), scale)
        factor[tile] = present[tile : tile + 1] * scale

    def piece(j, i):
        lanes = pl.ds(pl.multiple_of(2 * LANES * (i // PARTS), 2 * LANES), 2 * LANES)
        part_of = i % PARTS
        return mine.at[2 * j + part_of // 2, pl.ds(2 * (part_of % 2), 2), :, lanes]

    def give(source, target, send_sem, recv_sem, peer):
        return pltpu.make_async_remote_copy(
            src_ref=source, dst_ref=target, send_sem=send_sem, recv_sem=recv_sem,
            device_id=peer, device_id_type=MESH,
        )

    side = col // (NZ * NX // 2)
    is_source = col % (NZ * NX // 2) == 0
    at_home = distance(side, row) == 0
    shifted = moved(side, row)
    plain = both(jnp.logical_not(at_home), jnp.logical_not(shifted))
    carries_x = both(x % 2 == 1, both(z % (NZ // 2) == 0, jnp.logical_not(at_home)))
    carries_y = both(is_source, moved(side, prior))
    carries_n = both(x == 3, both(z % (NZ // 2) == 0, at_home))
    base_col = side * (NZ * NX // 2)

    def root_copies(i):
        def to(j, target, recv_sem, peer):
            return give(piece(j, i), target, root_sem.at[i, j], recv_sem, peer)

        held = hold.at[0, i], hold_sem.at[0, i]
        held_too = hold.at[1, i], hold_sem.at[1, i]
        landed = land.at[side, i], land_sem.at[side, i]
        for j in (1, 3):
            yield jnp.logical_not(at_home), to(j, *held, (row, base_col + j))
            yield at_home, to(j, *landed, (row, base_col + j))
        yield plain, to(0, *landed, (row, row * NX))
        yield plain, to(2, *landed, (row, row * NX + 2))
        yield shifted, to(0, *held, along_y(1))
        yield shifted, to(2, *held_too, along_y(1))
        yield both(at_home, i % 2 == 0), to(2, *landed, (row, row * NX + 2))
        yield both(at_home, i % 2 == 1), to(2, *held_too, (row, base_col + 3))

    def relay_copies(i):
        for needed, kind, slot, target in (
            (carries_x, 0, 0, row * NX + x),
            (carries_y, 1, 0, prior * NX),
            (carries_y, 1, 1, prior * NX + 2),
            (both(carries_n, i % 2 == 1), 0, 1, row * NX + 2),
        ):
            yield needed, slot, give(
                hold.at[slot, i], land.at[side, i], relay_sem.at[kind, slot, i], land_sem.at[side, i], (row, target)
            )

    def all_sent(copies):
        for needed, copy in copies:

            @pl.when(needed)
            def _(copy=copy):
                copy.wait_send()

    def emit(i):
        @pl.when(is_source)
        def _():
            @pl.when(i >= DEEP)
            def _():
                all_sent(root_copies(i - DEEP))

            for needed, copy in root_copies(i):

                @pl.when(needed)
                def _(copy=copy):
                    copy.start()

            @pl.when(at_home)
            def _():
                pltpu.make_async_copy(piece(0, i), land.at[side, i], land_sem.at[side, i]).start()

    for q in range(WAVES):
        fetches[q].wait()

        def decode(zd, _, q=q):
            f = factor[zd // 2, :, LANES * q : LANES * (q + 1)]
            for half in range(2):
                value = raw[half, zd, :, :, LANES * q : LANES * (q + 1)].astype(jnp.float32)
                start = 2 * LANES * q + LANES * half
                mine[zd, :, :, start : start + LANES] = (value * f[None]).astype(jnp.bfloat16)
            return _

        lax.fori_loop(0, NZ, decode, 0)
        if q == 0:
            pl.semaphore_wait(barrier, expected)
            for i in range(DEEP):
                emit(jnp.int32(i))

    carries = jnp.logical_or(carries_x, jnp.logical_or(carries_y, carries_n))

    def relay(i):
        @pl.when(carries)
        def _():
            for needed, slot, copy in relay_copies(i):

                @pl.when(needed)
                def _(copy=copy, slot=slot):
                    pltpu.make_async_copy(hold.at[slot, i], hold.at[slot, i], hold_sem.at[slot, i]).wait()
                    copy.start()

    busy = [both(x == 0, distance(p, z) == 0) for p in range(2)]

    def passes(p, i):
        pull = i % 2
        up = both(jnp.logical_not(busy[p]), jnp.logical_or(dy[p] == 0, both(dy[p] == 1, pull == 0)))
        down = jnp.logical_or(dy[p] == 0, both(dy[p] == NY - 1, pull == 1))
        down = jnp.where(busy[p], dy[p] != 1, down)
        for slot, (needed, peer) in enumerate(((up, along_y(1)), (down, along_y(-1)), (dy[p] >= 0, other))):
            copy = give(land.at[p, i], land.at[p, i], pass_sem.at[p, i, slot], land_sem.at[p, i], peer)
            yield needed, copy

    def hops(p):
        even = jnp.where(distance(p, z) == 0, jnp.where(x == 0, 0, 2), jnp.where(moved(p, z), 2, 1))
        at_first = jnp.where(odd, jnp.where(distance(p, z) == 0, 1, 2), even)
        return at_first + jnp.where(both(dy[p] == 1, jnp.logical_not(busy[p])), 1, wrap(-dy[p], NY)) + 1 - match.astype(jnp.int32)

    away = [hops(p) for p in range(2)]

    def arrive(p, tick):
        late = tick - HOP * away[p]
        i = late // PACE

        @pl.when(both(both(late >= 0, late % PACE == 0), i < ITEMS))
        def _():
            pltpu.make_async_copy(land.at[p, i], land.at[p, i], land_sem.at[p, i]).wait()

            @pl.when(match)
            def _():
                for needed, copy in passes(p, i):

                    @pl.when(needed)
                    def _(copy=copy):
                        copy.start()

    def build(p, q):
        for k in range(4):
            block = land[p, PARTS * q + k].reshape(LANES, 2 * LANES)
            real, imag = block[:, :LANES], block[:, LANES:]
            at = 2 * LANES * k
            rhs[q, p, at : at + LANES, :] = block
            rhs[q, p, at + LANES : at + 2 * LANES, :LANES] = -imag
            rhs[q, p, at + LANES : at + 2 * LANES, LANES:] = real

    def product(w, p, rows):
        return jnp.dot(rows.reshape(8 * 64, 8 * LANES), rhs[w, p], preferred_element_type=jnp.float32)

    def multiply_z(slot, which, start, count):
        def block(k, _):
            pair = [wrap(z + NZ // 2 + 2 * k + i, NZ) for i in range(2)]
            rows = jnp.concatenate([mine[zd] for zd in pair], axis=0)
            terms = product(slot, which, rows).reshape(2, 4, 64, 2 * LANES)
            for i, zd in enumerate(pair):
                part[slot, which, zd] = terms[i]
            return _

        lax.fori_loop(start, start + count, block, 0)

    def multiply_x(slot, which, start, count):
        def block(k, _):
            xd = wrap(x + NX // 2 + k, NX)
            part[slot, which, :, xd] = product(slot, which, mine[:, xd]).reshape(8, 64, 2 * LANES)
            return _

        lax.fori_loop(start, start + count, block, 0)

    def chains(group):
        w, which, kind, nth = group // 2, group % 2, KINDS[group], KINDS[:group].count(KINDS[group])
        if kind == "Z":
            first = Chain(
                NZ, z, along_z, lambda d, g: part[w, which, d, g], NX, True,
                z_send.at[nth], z_recv.at[nth], z_ss.at[nth], z_rs.at[nth],
            )
            then = Chain(
                NX, x, along_x, lambda d, g: summed[w, which, d, g], 2, False,
                zx_send.at[nth], zx_recv.at[nth], zx_ss.at[nth], zx_rs.at[nth],
            )
        else:
            first = Chain(
                NX, x, along_x, lambda d, g: part[w, which, g, d], NZ, True,
                x_send.at[nth], x_recv.at[nth], x_ss.at[nth], x_rs.at[nth],
            )
            then = Chain(
                NZ, z, along_z, lambda d, g: summed[w, which, d, g], 2, False,
                xz_send.at[nth], xz_recv.at[nth], xz_ss.at[nth], xz_rs.at[nth],
            )
        return first, then

    all_chains = [chains(group) for group in range(2 * WAVES)]

    def keep(slot, which):
        def put(g, value):
            summed[slot, which, g] = value.reshape(2, 32, 2 * LANES)

        return put

    def result(p, w):
        def put(g, value):
            value = value.astype(jnp.bfloat16)
            for half in range(2):
                out_ref[p, half, pl.ds(pl.multiple_of(32 * g, 32), 32), LANES * w : LANES * (w + 1)] = value[
                    :, LANES * half : LANES * (half + 1)
                ]

        return put

    def run(group, op):
        w, which = group // 2, group % 2
        first, then = all_chains[group]
        multiply = multiply_z if KINDS[group] == "Z" else multiply_x
        if op == "H":
            build(which, w)
            multiply(w, which, 0, 1)
            first.step(0)
        elif op == "M":
            multiply(w, which, 1, 3)
            first.step(EARLY)
        elif op == "f":
            first.finish(keep(w, which))
            then.step(0)
        elif op == "F":
            then.finish(result(which, w))
        else:
            (first if op[0] == "s" else then).step(int(op[1]))

    def spread(tick, carry):
        i = tick // PACE

        @pl.when(both(tick % PACE == 0, both(i >= DEEP, i < ITEMS)))
        def _():
            emit(i)

        held = (tick - HOP) // PACE

        @pl.when(both((tick - HOP) % PACE == 0, both(tick >= HOP, held < ITEMS)))
        def _():
            relay(held)

        for p in range(2):
            arrive(p, tick)
        return carry

    def settle(i, carry):
        @pl.when(match)
        def _():
            for p in range(2):
                all_sent(passes(p, i))

        @pl.when(carries)
        def _():
            all_sent((needed, copy) for needed, _, copy in relay_copies(i))

        @pl.when(both(is_source, i >= ITEMS - DEEP))
        def _():
            all_sent(root_copies(i))

        return carry

    tick = 0
    for token in ORDER:
        if isinstance(token, int):
            lax.fori_loop(tick, token, spread, 0)
            tick = token
        elif token == "settle":
            lax.fori_loop(0, ITEMS, settle, 0)
        elif token[1:] == "drain":
            for chain in all_chains[int(token[0])]:
                chain.drain()
        else:
            run(int(token[0]), token[1:])


def on_device(raw_blocks, occupancy, exponent):
    bf16, f32 = jnp.bfloat16, jnp.float32
    dma = pltpu.SemaphoreType.DMA
    n = 2 * LANES
    return pl.pallas_call(
        kernel,
        out_shape=jax.ShapeDtypeStruct((2, 2, 64, 512), bf16),
        in_specs=[
            pl.BlockSpec(memory_space=pl.ANY),
            pl.BlockSpec(memory_space=pltpu.VMEM),
            pl.BlockSpec(memory_space=pl.ANY),
        ],
        out_specs=pl.BlockSpec(memory_space=pltpu.VMEM),
        scratch_shapes=[
            pltpu.SMEM((4, 1), jnp.int32),
            dma,
            pltpu.VMEM((2, NZ, NX, 64, 512), bf16),
            pltpu.VMEM((4, 1, 512), f32),
            pltpu.VMEM((NZ, NX, 64, 1024), bf16),
            pltpu.VMEM((2, ITEMS, 2, 64, n), bf16),
            pltpu.VMEM((2, ITEMS, 2, 64, n), bf16),
            pltpu.VMEM((WAVES, 2, 1024, n), bf16),
            pltpu.VMEM((WAVES, 2, NZ, NX, 64, n), f32),
            pltpu.VMEM((WAVES, 2, NZ, 2, 32, n), f32),
            pltpu.VMEM((NUM_Z, 2, NZ // 2, NX, 64, n), bf16),
            pltpu.VMEM((NUM_Z, 2, NZ // 2, NX, 64, n), bf16),
            pltpu.VMEM((NUM_X, 2, NX // 2, NZ, 64, n), bf16),
            pltpu.VMEM((NUM_X, 2, NX // 2, NZ, 64, n), bf16),
            pltpu.VMEM((NUM_Z, 2, NX // 2, 2, 32, n), bf16),
            pltpu.VMEM((NUM_Z, 2, NX // 2, 2, 32, n), bf16),
            pltpu.VMEM((NUM_X, 2, NZ // 2, 2, 32, n), bf16),
            pltpu.VMEM((NUM_X, 2, NZ // 2, 2, 32, n), bf16),
            dma((WAVES,)),
            dma((ITEMS, NX)),
            dma((2, ITEMS)),
            dma((2, ITEMS)),
            dma((2, 2, ITEMS)),
            dma((2, ITEMS, 3)),
            dma((NUM_Z, 2, NZ // 2 + 1)),
            dma((NUM_Z, 2, NZ // 2 + 1)),
            dma((NUM_X, 2, NX // 2 + 1)),
            dma((NUM_X, 2, NX // 2 + 1)),
            dma((NUM_Z, 2, NX // 2)),
            dma((NUM_Z, 2, NX // 2)),
            dma((NUM_X, 2, NZ // 2)),
            dma((NUM_X, 2, NZ // 2)),
        ],
        compiler_params=pltpu.CompilerParams(
            collective_id=0, has_side_effects=True, vmem_limit_bytes=60 * 2**20
        ),
    )(raw_blocks.reshape(2, NZ, NX, 64, 512), occupancy, exponent)


def solution(mesh):
    placed = (P(None, "row", "col"), P("row", "col"), P("row", "col"))
    return jax.shard_map(
        on_device,
        mesh=mesh,
        in_specs=placed,
        out_specs=P(None, None, ("row", "col"), None),
        check_vma=False,
    )
```

```python
import functools

import jax
import jax.numpy as jnp
from jax import lax
from jax.experimental import pallas as pl
from jax.experimental.pallas import tpu as pltpu
from jax.sharding import PartitionSpec as P

MESH = pl.DeviceIdType.MESH
NY, NZ, NX = 4, 8, 4
WAVES = 4
LANES = 128
PARTS = 4
ITEMS = PARTS * WAVES
PACE = 2
HOP = 5
DEEP = 8
EARLY = 99
KINDS = "ZXZXZXZX"
NUM_Z, NUM_X = KINDS.count("Z"), KINDS.count("X")
ORDER = (
    32, "0H", "0M", 34, "1H", "1M", 36, "0s1", 40, "2H", "1s1", 41, "2M", 42, "0s2", 43,
    "3H", "3M", 45, "2s1", 48, "4H", "4M", 50, "0s3", "1f", 51, "5H", "5M", 53, "2s2", "4s1",
    54, "3s1", 56, "7H", "6H", "0f", "5s1", "1t1", "6M", "7M", "2s3", "4s2", "3f", "6s1", "1t2", "7s1",
    "0t1", "2f", "4s3", "3t1", "5f", "6s2", "1t3", "4f", "7f", "3t2", "5t1", "0F", "2t1", "4t1", "6s3", "2F",
    "1F", "7t1", "3t3", "4F", "5t2", "6f", "7t2", "3F", "settle", "0drain", "1drain", "2drain", "3drain", "4drain", "5t3", "6t1",
    "7t3", "5F", "6F", "7F", "5drain", "6drain", "7drain",
)


def wrap(index, size):
    return lax.rem(index + size, size)


class Chain:
    def __init__(self, n, me, neighbour, own, groups, split, send, recv, send_sem, recv_sem):
        self.split = split
        self.n, self.me, self.neighbour, self.own, self.groups = n, me, neighbour, own, groups
        self.send, self.recv, self.send_sem, self.recv_sem = send, recv, send_sem, recv_sem
        self.started = []

    def half(self, side):
        size = self.groups // 2
        return pl.ds(size * side, size)

    def copy(self, side, step):
        if step == 0 or (self.split and step in (1, EARLY)):
            cut = self.half(1 - side if step == EARLY else side)
            at = min(step, 1)
            source, target = self.send.at[side, at, cut], self.recv.at[side, at, cut]
        else:
            source, target = self.send.at[side, step], self.recv.at[side, step]
        return pltpu.make_async_remote_copy(
            src_ref=source,
            dst_ref=target,
            send_sem=self.send_sem.at[side, min(step, self.n // 2)],
            recv_sem=self.recv_sem.at[side, min(step, self.n // 2)],
            device_id=self.neighbour(1 - 2 * side),
            device_id_type=MESH,
        )

    def landed(self, side, step):
        self.copy(side, step).wait_recv()
        if step == 1 and self.split:
            self.copy(side, EARLY).wait_recv()

    def step(self, step):
        for side in range(2):
            slot = min(step, 1) if step == EARLY else step
            away = self.n // 2 - slot
            dest = wrap(self.me + (1 - 2 * side) * away, self.n)
            size = self.groups // 2
            halves = (side, 1 - side) if step else (side,)
            if self.split and step == 1:
                halves = (side,)
            if step == EARLY:
                halves = (1 - side,)
            elif step:
                self.landed(side, step - 1)
            for part in halves:
                with_received = step != EARLY and (step > 1 or (step == 1 and part == side))

                def block(g, _, part=part, with_received=with_received, dest=dest, side=side, slot=slot):
                    at = part * size + g
                    value = self.own(dest, at)
                    if with_received:
                        value = value + self.recv[side, step - 1, at].astype(jnp.float32)
                    self.send[side, slot, at] = value.astype(jnp.bfloat16)
                    return _

                lax.fori_loop(0, size, block, 0)
            copy = self.copy(side, step)
            copy.start()
            self.started.append(copy)

    def finish(self, put):
        last = self.n // 2 - 1
        for side in range(2):
            self.landed(side, last)

        def block(g, _):
            value = self.own(self.me, g)
            for side in range(2):
                value = value + self.recv[side, last, g].astype(jnp.float32)
            put(g, value)
            return _

        lax.fori_loop(0, self.groups, block, 0)

    def drain(self):
        for copy in self.started:
            copy.wait_send()


def kernel(
    raw_ref, occ_ref, exp_ref, out_ref,
    power_of, power_sem, raw, factor, mine, land, hold, rhs, part, summed,
    z_send, z_recv, x_send, x_recv, zx_send, zx_recv, xz_send, xz_recv,
    raw_sem, root_sem, land_sem, hold_sem, relay_sem, pass_sem,
    z_ss, z_rs, x_ss, x_rs, zx_ss, zx_rs, xz_ss, xz_rs,
):
    row, col = lax.axis_index("row"), lax.axis_index("col")
    y, core, z, x = row // 2, row % 2, col // NX, col % NX

    def device(y, core, z, x):
        return (wrap(y, NY) * 2 + core, wrap(z, NZ) * NX + wrap(x, NX))

    def along_z(step):
        return device(y, core, z + step, x)

    def along_x(step):
        return device(y, core, z, x + step)

    def along_y(step):
        return device(y + step, core, z, x)

    other = device(y, 1 - core, z, x)
    fetches = [
        pltpu.make_async_copy(
            raw_ref.at[:, :, :, :, pl.ds(LANES * q, LANES)],
            raw.at[:, :, :, :, pl.ds(LANES * q, LANES)],
            raw_sem.at[q],
        )
        for q in range(WAVES)
    ]
    for fetch in fetches:
        fetch.start()

    barrier = pltpu.get_barrier_semaphore()
    for peer in (along_z(1), along_z(-1), along_x(1), along_x(-1), along_y(1), along_y(-1), other):
        pl.semaphore_signal(barrier, inc=1, device_id=peer, device_id_type=MESH)
    expected = jnp.int32(7)
    both = jnp.logical_and
    root_col = [p * (NZ * NX // 2) for p in range(2)]
    is_root = [col == c for c in root_col]
    odd = x % 2 == 1

    def distance(p, plane):
        return wrap(plane - p * (NZ // 2), NZ)

    def moved(p, plane):
        d = distance(p, plane)
        return jnp.logical_or(jnp.logical_or(d == 3, d == 4), d == 7)

    prior = wrap(row - 2, NZ)
    here = [distance(p, row) == 0 for p in range(2)]
    direct = [both(is_root[p], jnp.logical_not(moved(p, row))) for p in range(2)]
    relay_x = [
        both(jnp.logical_or(col == root_col[p] + 1, col == root_col[p] + 3), jnp.logical_not(here[p]))
        for p in range(2)
    ]
    relay_n = [both(col == root_col[p] + 3, here[p]) for p in range(2)]
    relay_y = [both(is_root[p], moved(p, prior)) for p in range(2)]
    match = core == z % 2
    dy = [wrap(y - z // 2 - both(jnp.logical_not(odd), moved(p, z)).astype(jnp.int32), NY) for p in range(2)]
    first = [both(match, dy[p] == 0) for p in range(2)]

    greet = []
    for p in range(2):
        greet.append((both(direct[p], jnp.logical_not(here[p])), row * NX))
        greet.append((direct[p], row * NX + 2))
        greet.append((relay_x[p], row * NX + x))
        greet.append((relay_y[p], prior * NX))
        greet.append((relay_y[p], prior * NX + 2))
        near = both(distance(p, z) == 0, x != 2)
        greet.append((both(first[p], jnp.logical_not(near)), root_col[p] + jnp.where(odd, x, 0)))
    for needed, peer in greet:
        expected = expected + needed.astype(jnp.int32)

        @pl.when(needed)
        def _(peer=peer):
            pl.semaphore_signal(barrier, inc=1, device_id=(row, peer), device_id_type=MESH)

    powers = pltpu.make_async_copy(exp_ref, power_of, power_sem)
    powers.start()
    powers.wait()
    present = occ_ref[...].astype(jnp.float32)
    for tile in range(NZ // 2):
        exponent = power_of[tile, 0]
        scale = jnp.float32(1.0)
        for power in (-2, -1, 1, 2):
            scale = jnp.where(exponent == power, jnp.float32(2.0**power), scale)
        factor[tile] = present[tile : tile + 1] * scale

    def piece(j, i):
        lanes = pl.ds(pl.multiple_of(2 * LANES * (i // PARTS), 2 * LANES), 2 * LANES)
        part_of = i % PARTS
        return mine.at[2 * j + part_of // 2, pl.ds(2 * (part_of % 2), 2), :, lanes]

    def give(source, target, send_sem, recv_sem, peer):
        return pltpu.make_async_remote_copy(
            src_ref=source, dst_ref=target, send_sem=send_sem, recv_sem=recv_sem,
            device_id=peer, device_id_type=MESH,
        )

    side = col // (NZ * NX // 2)
    is_source = col % (NZ * NX // 2) == 0
    at_home = distance(side, row) == 0
    shifted = moved(side, row)
    plain = both(jnp.logical_not(at_home), jnp.logical_not(shifted))
    carries_x = both(x % 2 == 1, both(z % (NZ // 2) == 0, jnp.logical_not(at_home)))
    carries_y = both(is_source, moved(side, prior))
    carries_n = both(x == 3, both(z % (NZ // 2) == 0, at_home))
    base_col = side * (NZ * NX // 2)

    def root_copies(i):
        def to(j, target, recv_sem, peer):
            return give(piece(j, i), target, root_sem.at[i, j], recv_sem, peer)

        held = hold.at[0, i], hold_sem.at[0, i]
        held_too = hold.at[1, i], hold_sem.at[1, i]
        landed = land.at[side, i], land_sem.at[side, i]
        for j in (1, 3):
            yield jnp.logical_not(at_home), to(j, *held, (row, base_col + j))
            yield at_home, to(j, *landed, (row, base_col + j))
        yield plain, to(0, *landed, (row, row * NX))
        yield plain, to(2, *landed, (row, row * NX + 2))
        yield shifted, to(0, *held, along_y(1))
        yield shifted, to(2, *held_too, along_y(1))
        yield both(at_home, i % 2 == 0), to(2, *landed, (row, row * NX + 2))
        yield both(at_home, i % 2 == 1), to(2, *held_too, (row, base_col + 3))

    def relay_copies(i):
        for needed, kind, slot, target in (
            (carries_x, 0, 0, row * NX + x),
            (carries_y, 1, 0, prior * NX),
            (carries_y, 1, 1, prior * NX + 2),
            (both(carries_n, i % 2 == 1), 0, 1, row * NX + 2),
        ):
            yield needed, slot, give(
                hold.at[slot, i], land.at[side, i], relay_sem.at[kind, slot, i], land_sem.at[side, i], (row, target)
            )

    def all_sent(copies):
        for needed, copy in copies:

            @pl.when(needed)
            def _(copy=copy):
                copy.wait_send()

    def emit(i):
        @pl.when(is_source)
        def _():
            @pl.when(i >= DEEP)
            def _():
                all_sent(root_copies(i - DEEP))

            for needed, copy in root_copies(i):

                @pl.when(needed)
                def _(copy=copy):
                    copy.start()

            @pl.when(at_home)
            def _():
                pltpu.make_async_copy(piece(0, i), land.at[side, i], land_sem.at[side, i]).start()

    for q in range(WAVES):
        fetches[q].wait()

        def decode(zd, _, q=q):
            f = factor[zd // 2, :, LANES * q : LANES * (q + 1)]
            for half in range(2):
                value = raw[half, zd, :, :, LANES * q : LANES * (q + 1)].astype(jnp.float32)
                start = 2 * LANES * q + LANES * half
                mine[zd, :, :, start : start + LANES] = (value * f[None]).astype(jnp.bfloat16)
            return _

        lax.fori_loop(0, NZ, decode, 0)
        if q == 0:
            pl.semaphore_wait(barrier, expected)
        for i in range(PARTS * q, min(PARTS * (q + 1), DEEP)):
            emit(jnp.int32(i))

    carries = jnp.logical_or(carries_x, jnp.logical_or(carries_y, carries_n))

    def relay(i):
        @pl.when(carries)
        def _():
            for needed, slot, copy in relay_copies(i):

                @pl.when(needed)
                def _(copy=copy, slot=slot):
                    pltpu.make_async_copy(hold.at[slot, i], hold.at[slot, i], hold_sem.at[slot, i]).wait()
                    copy.start()

    busy = [both(x == 0, distance(p, z) == 0) for p in range(2)]

    def passes(p, i):
        pull = i % 2
        up = both(jnp.logical_not(busy[p]), jnp.logical_or(dy[p] == 0, both(dy[p] == 1, pull == 0)))
        down = jnp.logical_or(dy[p] == 0, both(dy[p] == NY - 1, pull == 1))
        down = jnp.where(busy[p], dy[p] != 1, down)
        for slot, (needed, peer) in enumerate(((up, along_y(1)), (down, along_y(-1)), (dy[p] >= 0, other))):
            copy = give(land.at[p, i], land.at[p, i], pass_sem.at[p, i, slot], land_sem.at[p, i], peer)
            yield needed, copy

    def hops(p):
        even = jnp.where(distance(p, z) == 0, jnp.where(x == 0, 0, 2), jnp.where(moved(p, z), 2, 1))
        at_first = jnp.where(odd, jnp.where(distance(p, z) == 0, 1, 2), even)
        return at_first + jnp.where(both(dy[p] == 1, jnp.logical_not(busy[p])), 1, wrap(-dy[p], NY)) + 1 - match.astype(jnp.int32)

    away = [hops(p) for p in range(2)]

    def arrive(p, tick):
        late = tick - HOP * away[p]
        i = late // PACE

        @pl.when(both(both(late >= 0, late % PACE == 0), i < ITEMS))
        def _():
            pltpu.make_async_copy(land.at[p, i], land.at[p, i], land_sem.at[p, i]).wait()

            @pl.when(match)
            def _():
                for needed, copy in passes(p, i):

                    @pl.when(needed)
                    def _(copy=copy):
                        copy.start()

    def build(p, q):
        for k in range(4):
            block = land[p, PARTS * q + k].reshape(LANES, 2 * LANES)
            real, imag = block[:, :LANES], block[:, LANES:]
            at = 2 * LANES * k
            rhs[q, p, at : at + LANES, :] = block
            rhs[q, p, at + LANES : at + 2 * LANES, :LANES] = -imag
            rhs[q, p, at + LANES : at + 2 * LANES, LANES:] = real

    def product(w, p, rows):
        return jnp.dot(rows.reshape(8 * 64, 8 * LANES), rhs[w, p], preferred_element_type=jnp.float32)

    def multiply_z(slot, which, start, count):
        def block(k, _):
            pair = [wrap(z + NZ // 2 + 2 * k + i, NZ) for i in range(2)]
            rows = jnp.concatenate([mine[zd] for zd in pair], axis=0)
            terms = product(slot, which, rows).reshape(2, 4, 64, 2 * LANES)
            for i, zd in enumerate(pair):
                part[slot, which, zd] = terms[i]
            return _

        lax.fori_loop(start, start + count, block, 0)

    def multiply_x(slot, which, start, count):
        def block(k, _):
            xd = wrap(x + NX // 2 + k, NX)
            part[slot, which, :, xd] = product(slot, which, mine[:, xd]).reshape(8, 64, 2 * LANES)
            return _

        lax.fori_loop(start, start + count, block, 0)

    def chains(group):
        w, which, kind, nth = group // 2, group % 2, KINDS[group], KINDS[:group].count(KINDS[group])
        if kind == "Z":
            first = Chain(
                NZ, z, along_z, lambda d, g: part[w, which, d, g], NX, True,
                z_send.at[nth], z_recv.at[nth], z_ss.at[nth], z_rs.at[nth],
            )
            then = Chain(
                NX, x, along_x, lambda d, g: summed[w, which, d, g], 2, False,
                zx_send.at[nth], zx_recv.at[nth], zx_ss.at[nth], zx_rs.at[nth],
            )
        else:
            first = Chain(
                NX, x, along_x, lambda d, g: part[w, which, g, d], NZ, True,
                x_send.at[nth], x_recv.at[nth], x_ss.at[nth], x_rs.at[nth],
            )
            then = Chain(
                NZ, z, along_z, lambda d, g: summed[w, which, d, g], 2, False,
                xz_send.at[nth], xz_recv.at[nth], xz_ss.at[nth], xz_rs.at[nth],
            )
        return first, then

    all_chains = [chains(group) for group in range(2 * WAVES)]

    def keep(slot, which):
        def put(g, value):
            summed[slot, which, g] = value.reshape(2, 32, 2 * LANES)

        return put

    def result(p, w):
        def put(g, value):
            value = value.astype(jnp.bfloat16)
            for half in range(2):
                out_ref[p, half, pl.ds(pl.multiple_of(32 * g, 32), 32), LANES * w : LANES * (w + 1)] = value[
                    :, LANES * half : LANES * (half + 1)
                ]

        return put

    def run(group, op):
        w, which = group // 2, group % 2
        first, then = all_chains[group]
        multiply = multiply_z if KINDS[group] == "Z" else multiply_x
        if op == "H":
            build(which, w)
            multiply(w, which, 0, 1)
            first.step(0)
        elif op == "M":
            multiply(w, which, 1, 3)
            first.step(EARLY)
        elif op == "f":
            first.finish(keep(w, which))
            then.step(0)
        elif op == "F":
            then.finish(result(which, w))
        else:
            (first if op[0] == "s" else then).step(int(op[1]))

    def spread(tick, carry):
        i = tick // PACE

        @pl.when(both(tick % PACE == 0, both(i >= DEEP, i < ITEMS)))
        def _():
            emit(i)

        held = (tick - HOP) // PACE

        @pl.when(both((tick - HOP) % PACE == 0, both(tick >= HOP, held < ITEMS)))
        def _():
            relay(held)

        for p in range(2):
            arrive(p, tick)
        return carry

    def settle(i, carry):
        @pl.when(match)
        def _():
            for p in range(2):
                all_sent(passes(p, i))

        @pl.when(carries)
        def _():
            all_sent((needed, copy) for needed, _, copy in relay_copies(i))

        @pl.when(both(is_source, i >= ITEMS - DEEP))
        def _():
            all_sent(root_copies(i))

        return carry

    tick = 0
    for token in ORDER:
        if isinstance(token, int):
            lax.fori_loop(tick, token, spread, 0)
            tick = token
        elif token == "settle":
            lax.fori_loop(0, ITEMS, settle, 0)
        elif token[1:] == "drain":
            for chain in all_chains[int(token[0])]:
                chain.drain()
        else:
            run(int(token[0]), token[1:])


def on_device(raw_blocks, occupancy, exponent):
    bf16, f32 = jnp.bfloat16, jnp.float32
    dma = pltpu.SemaphoreType.DMA
    n = 2 * LANES
    return pl.pallas_call(
        kernel,
        out_shape=jax.ShapeDtypeStruct((2, 2, 64, 512), bf16),
        in_specs=[
            pl.BlockSpec(memory_space=pl.ANY),
            pl.BlockSpec(memory_space=pltpu.VMEM),
            pl.BlockSpec(memory_space=pl.ANY),
        ],
        out_specs=pl.BlockSpec(memory_space=pltpu.VMEM),
        scratch_shapes=[
            pltpu.SMEM((4, 1), jnp.int32),
            dma,
            pltpu.VMEM((2, NZ, NX, 64, 512), bf16),
            pltpu.VMEM((4, 1, 512), f32),
            pltpu.VMEM((NZ, NX, 64, 1024), bf16),
            pltpu.VMEM((2, ITEMS, 2, 64, n), bf16),
            pltpu.VMEM((2, ITEMS, 2, 64, n), bf16),
            pltpu.VMEM((WAVES, 2, 1024, n), bf16),
            pltpu.VMEM((WAVES, 2, NZ, NX, 64, n), f32),
            pltpu.VMEM((WAVES, 2, NZ, 2, 32, n), f32),
            pltpu.VMEM((NUM_Z, 2, NZ // 2, NX, 64, n), bf16),
            pltpu.VMEM((NUM_Z, 2, NZ // 2, NX, 64, n), bf16),
            pltpu.VMEM((NUM_X, 2, NX // 2, NZ, 64, n), bf16),
            pltpu.VMEM((NUM_X, 2, NX // 2, NZ, 64, n), bf16),
            pltpu.VMEM((NUM_Z, 2, NX // 2, 2, 32, n), bf16),
            pltpu.VMEM((NUM_Z, 2, NX // 2, 2, 32, n), bf16),
            pltpu.VMEM((NUM_X, 2, NZ // 2, 2, 32, n), bf16),
            pltpu.VMEM((NUM_X, 2, NZ // 2, 2, 32, n), bf16),
            dma((WAVES,)),
            dma((ITEMS, NX)),
            dma((2, ITEMS)),
            dma((2, ITEMS)),
            dma((2, 2, ITEMS)),
            dma((2, ITEMS, 3)),
            dma((NUM_Z, 2, NZ // 2 + 1)),
            dma((NUM_Z, 2, NZ // 2 + 1)),
            dma((NUM_X, 2, NX // 2 + 1)),
            dma((NUM_X, 2, NX // 2 + 1)),
            dma((NUM_Z, 2, NX // 2)),
            dma((NUM_Z, 2, NX // 2)),
            dma((NUM_X, 2, NZ // 2)),
            dma((NUM_X, 2, NZ // 2)),
        ],
        compiler_params=pltpu.CompilerParams(
            collective_id=0, has_side_effects=True, vmem_limit_bytes=60 * 2**20
        ),
    )(raw_blocks.reshape(2, NZ, NX, 64, 512), occupancy, exponent)


def solution(mesh):
    placed = (P(None, "row", "col"), P("row", "col"), P("row", "col"))
    return jax.shard_map(
        on_device,
        mesh=mesh,
        in_specs=placed,
        out_specs=P(None, None, ("row", "col"), None),
        check_vma=False,
    )
```
